32 devices in a mesh: group: 2 (over y), cable: 8 (over z, x), fold: 2 (over core).
Axes of the slice: x: 2, y: 2, z: 4, core: 2. Of those that a mesh axis runs over, the one named last changes fastest.
Arguments:
- raw: bfloat16 [16, 1024, 1024], P(('group', 'fold'), None, 'cable'), parts along dimension 0, as said below
- seg_count: int32 [32], P('group'), parts along dimension 0, may hold values from 4 to 8
- mask: int32 [2048], P(('group', 'cable')), parts along dimension 0, may hold values 0 or 1
Outputs:
- xcorr: float32 [16, 101, 1024], P(('group', 'fold'), None, 'cable'), parts along dimension 0
The draws below stay inside these ranges and needn't reach their ends.
There are 2 independent parts, one for each index of `group`. The reference program is written for one: setup_inputs(seed, part) draws one part's arguments, and reference() takes and returns one part's arrays. A program takes and returns all parts, laid end to end along the dimension named above; each array names one. Nothing has to cross between parts.
Inputs may be any that keep to these rules, and one draw needn't show every extreme that they name: raw has a scale of its own for each segment and channel.
All inputs are finite; a program needn't handle non-finite values. No bound on the sum of `mask` on one device may be relied on, other than what follows from the above.
Results may differ from the reference program's by a relative error of at most 0.0066.
Values may be sent and summed in bfloat16 or wider, within the bound.
A program may use at most 64 MiB of HBM per device.

```python
import math
import jax
import jax.numpy as jnp
from jax import lax

CHAN_BLK = 64
SAMPLES = 1024
LAGS = 101
NOFF = 8
BINS = 512
SEG = 8
NBLK = 16
CHANNELS = 1024


def draw_raw(key, part):
    key = jax.random.fold_in(key, 11)
    first, second = jax.random.split(key)
    noise = jax.random.normal(first, (SEG, SAMPLES, CHANNELS), jnp.float32)
    logs = jax.random.uniform(second, (SEG, 1, CHANNELS), jnp.float32, math.log(0.3), math.log(3.0))
    return (noise * jnp.exp(logs)).astype(jnp.bfloat16)


def plant(entries, own_key, low, high):
    place = [jax.random.randint(jax.random.fold_in(own_key, axis), (), 0, length) for axis, length in enumerate(entries.shape)]
    longest = entries.shape.index(max(entries.shape))
    neighbour = place[:longest] + [(place[longest] + 1) % entries.shape[longest]] + place[longest + 1:]
    return entries.at[tuple(place)].set(low).at[tuple(neighbour)].set(high)


def setup_inputs(seed: int = 0, part: int = 0) -> dict:
    key_of = jax.random.split(jax.random.key(seed), 4)
    own_keys = jax.random.split(jax.random.fold_in(key_of[3], part), 4)
    return {
        "raw": draw_raw(jax.random.fold_in(jax.random.fold_in(key_of[3], part), 71), part),
        "seg_count": plant(jax.random.randint(own_keys[1], (NBLK,), SEG // 2, SEG + 1), jax.random.fold_in(own_keys[1], 1), SEG // 2, SEG).astype(jnp.int32),
        "mask": plant((jax.random.randint(own_keys[2], (CHANNELS,), 0, 8) < 7).astype(jnp.int32), jax.random.fold_in(own_keys[2], 1), 0, 1),
    }


def forward_table(samples, bins):
    times = jnp.arange(samples, dtype=jnp.int32)
    freqs = jnp.arange(bins, dtype=jnp.int32)
    phase = (times[:, None] * freqs[None, :] % samples).astype(jnp.float32) * (2.0 * math.pi / samples)
    return jnp.concatenate([jnp.cos(phase), -jnp.sin(phase)], axis=1).astype(jnp.bfloat16)

def lag_table(samples, bins, lags):
    freqs = jnp.arange(bins, dtype=jnp.int32)
    offsets = jnp.arange(lags, dtype=jnp.int32) - lags // 2 + samples
    phase = (freqs[:, None] * offsets[None, :] % samples).astype(jnp.float32) * (2.0 * math.pi / samples)
    return jnp.concatenate([jnp.cos(phase), -jnp.sin(phase)], axis=0) / math.sqrt(bins)

def normalize(record, axis):
    values = record.astype(jnp.float32)
    spread = jnp.sqrt(lax.optimization_barrier(jnp.mean(values * values, axis=axis, keepdims=True)) + 1e-06)
    return (jnp.clip(values, -2.0 * spread, 2.0 * spread) / spread).astype(jnp.bfloat16)

def whiten(spectrum, usable, bins):
    real_part = spectrum[..., :bins, :]
    imag_part = spectrum[..., bins:, :]
    power = real_part * real_part + imag_part * imag_part
    widths = ((0, 0),) * (power.ndim - 2) + ((2, 2), (0, 0))
    padded = jnp.pad(power, widths)
    smooth = (padded[..., 0:bins, :] + padded[..., 1:bins + 1, :] + padded[..., 2:bins + 2, :] + padded[..., 3:bins + 3, :] + padded[..., 4:bins + 4, :]) / 5.0
    level = smooth + 0.01 * lax.optimization_barrier(jnp.mean(power, axis=-2, keepdims=True))
    factor = usable / jnp.sqrt(level)
    return jnp.concatenate([real_part * factor, imag_part * factor], axis=-2).astype(jnp.bfloat16)

def cross(first, second, bins):
    left = first.astype(jnp.float32)
    right = second.astype(jnp.float32)
    left_re, left_im = (left[..., :bins, :], left[..., bins:, :])
    right_re, right_im = (right[..., :bins, :], right[..., bins:, :])
    return jnp.concatenate([left_re * right_re + left_im * right_im, left_im * right_re - left_re * right_im], axis=-2)

def reference(raw, seg_count, mask):
    table = forward_table(SAMPLES, BINS)
    usable = mask.astype(jnp.float32)
    chan_count = jnp.repeat(seg_count, CHAN_BLK)
    padded_count = jnp.concatenate([chan_count, jnp.zeros((NOFF * CHAN_BLK,), jnp.int32)])
    pair_count = jnp.stack([jnp.minimum(chan_count, padded_count[k * CHAN_BLK:k * CHAN_BLK + CHANNELS]) for k in range(1, NOFF + 1)])
    divisor = jnp.maximum(pair_count, 1).astype(jnp.float32)

    def step(stack, item):
        segment, index = item
        clipped = normalize(segment, 0)
        spectrum = jnp.dot(table.T, clipped, preferred_element_type=jnp.float32)
        white = whiten(spectrum, usable, BINS)
        wide = jnp.concatenate([white, jnp.zeros((2 * BINS, NOFF * CHAN_BLK), jnp.bfloat16)], axis=1)
        terms = []
        for k in range(1, NOFF + 1):
            other = wide[:, k * CHAN_BLK:k * CHAN_BLK + CHANNELS]
            weight = (index < pair_count[k - 1]).astype(jnp.float32)
            terms.append(cross(white, other, BINS) * weight[None, :])
        return (stack + jnp.stack(terms), None)
    start = jnp.zeros((NOFF, 2 * BINS, CHANNELS), jnp.float32)
    stack, unused = lax.scan(step, start, (raw, jnp.arange(SEG, dtype=jnp.int32)))
    stack = stack / divisor[:, None, :]
    inverse = lag_table(SAMPLES, BINS, LAGS)
    return jnp.einsum('kgc,gl->klc', stack, inverse, precision=lax.Precision.HIGHEST)
```

```python
import functools
import math

import jax
import jax.numpy as jnp
import ml_dtypes
import numpy as np
from jax import lax
from jax.experimental import pallas as pl
from jax.experimental.pallas import tpu as pltpu
from jax.sharding import PartitionSpec as P

CHAN_BLK = 64
LAGS = 101
ROWS = 112
NOFF = 8
HALF = NOFF // 2
F32 = jnp.float32
BF16 = jnp.bfloat16
MESH = pl.DeviceIdType.MESH


def forward_table(samples):
    bins = samples // 2
    phase = np.outer(np.arange(bins), np.arange(samples)) % samples * (2.0 * math.pi / samples)
    return np.concatenate([np.cos(phase), -np.sin(phase)], axis=0).astype(ml_dtypes.bfloat16)


def lag_table(samples):
    bins = samples // 2
    lag = np.arange(LAGS) - LAGS // 2 + samples
    phase = np.outer(lag, np.arange(bins)) % samples * (2.0 * math.pi / samples)
    table = np.concatenate([np.cos(phase), -np.sin(phase)], axis=1) / math.sqrt(bins)
    full = np.zeros((ROWS, samples), np.float64)
    full[:LAGS] = table
    return full.astype(ml_dtypes.bfloat16)


MID = [(0, 7), (0, 8), (1, 5), (1, 6), (1, 7), (1, 8)]
HOME = [(0, 5), (0, 6), (0, 7), (1, 5), (0, 1), (0, 2), (0, 3), (0, 4), (1, 1), (1, 2), (1, 3), (1, 4)]


def kernel(
    size,
    raw, mask, cnt, basis_hbm, inv,
    out,
    basis, own_raw, nb_raw, mask_out, mask_in, spec, power, w0, wu, wl, prods, acc,
    home, mid, home_in, mid_in, hsend, msend, hrecv, mrecv,
    load_sem, xs, xr, us, ur, ds, dr, cs, cr, es, er, ms, mr,
):
    samples = raw.shape[1]
    bins = samples // 2
    cable = lax.axis_index("cable")
    fold = lax.axis_index("fold")
    side = cable % 2
    node = cable // 2
    has_up = node < size // 2 - 1
    has_dn = node > 0
    peer = cable + 1 - 2 * side
    nblk = cnt.shape[0]
    seg_dev = raw.shape[0]
    kept = seg_dev // 2

    def remote(src, dst, ssem, rsem, at, core):
        return pltpu.make_async_remote_copy(
            src_ref=src, dst_ref=dst, send_sem=ssem, recv_sem=rsem,
            device_id={"cable": at, "fold": core}, device_id_type=MESH,
        )

    raw_load = [
        pltpu.make_async_copy(raw.at[kept * side + s], own_raw.at[s], load_sem.at[s])
        for s in range(kept)
    ]
    basis_load = pltpu.make_async_copy(basis_hbm, basis, load_sem.at[kept])
    raw_load[0].start()
    basis_load.start()
    for s in range(1, kept):
        raw_load[s].start()
    mask_out[...] = jnp.broadcast_to(mask[...], mask_out.shape)

    barrier = pltpu.get_barrier_semaphore()

    def greet(at, core):
        pl.semaphore_signal(barrier, inc=1, device_id={"cable": at, "fold": core}, device_id_type=MESH)

    greet(peer, fold)
    greet(cable, 1 - fold)

    @pl.when(has_up)
    def _():
        greet(cable + 2, fold)
        greet(peer + 2, fold)

    @pl.when(has_dn)
    def _():
        greet(cable - 2, fold)
        greet(peer - 2, fold)

    peers = 2 + jnp.where(has_up, 2, 0) + jnp.where(has_dn, 2, 0)
    pl.semaphore_wait(barrier, peers)

    x_raw = [
        remote(raw.at[kept * (1 - side) + s], nb_raw.at[s], xs.at[s], xr.at[s], peer, fold)
        for s in range(kept)
    ]
    x_mask = remote(mask_out, mask_in, xs.at[kept], xr.at[kept], peer, fold)
    x_mask.start()
    for copy in x_raw:
        copy.start()

    power[0:8, :] = jnp.zeros((8, 128), F32)
    power[bins + 8 : bins + 16, :] = jnp.zeros((8, 128), F32)
    zero_tile = jnp.zeros((ROWS, 128), BF16)
    home[1, 0, 3] = zero_tile
    for kk in range(1, 4):
        home[1, 1, kk] = zero_tile
    mid[0, 0] = zero_tile
    mid[0, 1] = zero_tile

    @pl.when(jnp.logical_not(has_up))
    def _():
        @pl.loop(0, bins * 2 // 64)
        def _(t):
            at = pl.ds(pl.multiple_of(t * 64, 64), 64)
            for s in range(kept):
                for col in range(2):
                    wu[s, col, at, :] = jnp.zeros((64, 128), BF16)

    @pl.when(jnp.logical_not(has_dn))
    def _():
        @pl.loop(0, bins * 2 // 64)
        def _(t):
            at = pl.ds(pl.multiple_of(t * 64, 64), 64)
            for s in range(kept):
                for col in range(2):
                    wl[s, col, at, :] = jnp.zeros((64, 128), BF16)

    lane = lax.broadcasted_iota(jnp.int32, (1, 128), 1)
    low = lane < CHAN_BLK

    def whiten(source, usable, owner, s, dst):
        seg = fold * seg_dev + kept * side + s
        count = jnp.where(low, cnt[2 * owner], cnt[2 * owner + 1])
        keep = jnp.where(seg < count, usable.astype(F32), 0.0)

        def squares(t, total):
            v = source[pl.ds(pl.multiple_of(t * 64, 64), 64), :].astype(F32)
            return total + jnp.sum((v * v).reshape(8, 8, 128), axis=0)

        total = lax.fori_loop(0, samples // 64, squares, jnp.zeros((8, 128), F32))
        mean = jnp.sum(total, axis=0, keepdims=True) * (1.0 / samples)
        rate = lax.rsqrt(mean + 1e-06)
        clipped = jnp.clip(source[...].astype(F32) * rate, -2.0, 2.0).astype(BF16)

        @pl.loop(0, samples // 256)
        def _(t):
            at = pl.ds(pl.multiple_of(t * 256, 256), 256)
            spec[at, :] = jnp.dot(basis[at, :], clipped, preferred_element_type=F32)

        def powers(t, total):
            at = pl.multiple_of(t * 64, 64)
            re = spec[pl.ds(at, 64), :]
            im = spec[pl.ds(bins + at, 64), :]
            p = re * re + im * im
            power[pl.ds(8 + at, 64), :] = p
            return total + jnp.sum(p.reshape(8, 8, 128), axis=0)

        total = lax.fori_loop(0, bins // 64, powers, jnp.zeros((8, 128), F32))
        floor = jnp.sum(total, axis=0, keepdims=True) * (0.01 / bins)

        @pl.loop(0, bins // 64)
        def _(t):
            at = pl.multiple_of(t * 64, 64)
            wide = power[pl.ds(at, 80), :]
            smooth = wide[6:70] + wide[7:71] + wide[8:72] + wide[9:73] + wide[10:74]
            factor = keep * lax.rsqrt(smooth * 0.2 + floor)
            dst[pl.ds(at, 64), :] = (spec[pl.ds(at, 64), :] * factor).astype(BF16)
            dst[pl.ds(bins + at, 64), :] = (spec[pl.ds(bins + at, 64), :] * factor).astype(BF16)

    def chunk_copies(q, s, col):
        up = remote(w0.at[s, col], wl.at[s, col], us.at[q], dr.at[q], cable + 2, fold)
        dn = remote(w0.at[s, col], wu.at[s, col], ds.at[q], ur.at[q], cable - 2, fold)
        return up, dn

    def send(q, s, col):
        up, dn = chunk_copies(q, s, col)

        @pl.when(has_up)
        def _():
            up.start()

        @pl.when(has_dn)
        def _():
            dn.start()

    def arrive(q, s, col):
        up, dn = chunk_copies(q, s, col)

        @pl.when(has_dn)
        def _():
            up.wait_recv()

        @pl.when(has_up)
        def _():
            dn.wait_recv()

    def crosses(s):
        @pl.loop(0, bins // 16)
        def _(t):
            at = pl.multiple_of(t * 16, 16)

            def load(ref, col):
                return (
                    ref[s, col, pl.ds(at, 16), :].astype(F32),
                    ref[s, col, pl.ds(bins + at, 16), :].astype(F32),
                )

            e0, e1 = load(w0, 0), load(w0, 1)
            u0, u1 = load(wu, 0), load(wu, 1)
            l0, l1 = load(wl, 0), load(wl, 1)
            swap = lambda pair: tuple(pltpu.roll(v, CHAN_BLK, 1) for v in pair)
            join = lambda a, b: tuple(jnp.where(low, p, q) for p, q in zip(a, b))
            zero = (jnp.zeros((16, 128), F32),) * 2
            re0, re1, ru0, ru1 = swap(e0), swap(e1), swap(u0), swap(u1)
            o0, o1, o2, o3 = join(re0, re1), join(re1, ru0), join(ru0, ru1), join(ru1, zero)
            v0 = join(zero, ru0)
            ext = {(0, 1): o0, (0, 2): e1, (0, 3): o1, (0, 4): u0, (0, 5): o2, (0, 6): u1, (0, 7): o3,
                   (1, 1): o1, (1, 2): u0, (1, 3): o2, (1, 4): u1, (1, 5): o3}
            far = {(0, 7): v0, (0, 8): u0, (1, 5): v0, (1, 6): u0, (1, 7): o2, (1, 8): u1}
            jobs = [((l0, l1)[key[0]], far[key]) for key in MID]
            jobs += [((e0, e1)[key[0]], ext[key]) for key in HOME]
            for i, (a, b) in enumerate(jobs):
                lanes = slice(i % 2 * 128, i % 2 * 128 + 128)
                prods[i // 2, pl.ds(at, 16), lanes] = (a[0] * b[0] + a[1] * b[1]).astype(BF16)
                prods[i // 2, pl.ds(bins + at, 16), lanes] = (a[1] * b[0] - a[0] * b[1]).astype(BF16)

    def slot(i):
        if i < len(MID):
            col, k = MID[i]
            return mid.at[col, k - 1 - HALF]
        col, k = HOME[i - len(MID)]
        return home.at[(k - 1) // HALF, col, (k - 1) % HALF]

    def lags(i):
        return jnp.dot(inv[...], prods[i], preferred_element_type=F32)

    own_at, nb_at = side, 1 - side
    raw_load[0].wait()
    basis_load.wait()
    whiten(own_raw.at[0], mask[...], cable, 0, w0.at[0, own_at])
    send(0, 0, own_at)
    raw_load[1].wait()
    whiten(own_raw.at[1], mask[...], cable, 1, w0.at[1, own_at])
    x_mask.wait_recv()
    x_raw[0].wait_recv()
    whiten(nb_raw.at[0], mask_in[0:1, :], peer, 0, w0.at[0, nb_at])
    send(1, 0, nb_at)
    send(2, 1, own_at)
    x_raw[1].wait_recv()
    whiten(nb_raw.at[1], mask_in[0:1, :], peer, 1, w0.at[1, nb_at])
    send(3, 1, nb_at)

    arrive(0, 0, own_at)
    arrive(1, 0, nb_at)
    crosses(0)
    for i in range(9):
        acc[i] = lags(i)
    arrive(2, 1, own_at)
    arrive(3, 1, nb_at)
    crosses(1)

    def finish(i):
        total = acc[i] + lags(i)
        slot(2 * i)[...] = total[:, :128].astype(BF16)
        slot(2 * i + 1)[...] = total[:, 128:].astype(BF16)

    for i in range(3):
        finish(i)
    c_mid = remote(mid, mid_in, cs.at[0], cr.at[0], cable, 1 - fold)

    @pl.when(fold == 0)
    def _():
        c_mid.start()

    for i in range(3, 9):
        finish(i)
    c_home = remote(home.at[1 - fold], home_in, cs.at[1], cr.at[1], cable, 1 - fold)
    c_home.start()

    m_near = remote(msend.at[side], mrecv.at[0], ms.at[0], mr.at[0], cable - 2, fold)
    m_diag = remote(msend.at[1 - side], mrecv.at[1], ms.at[1], mr.at[1], peer - 2, fold)

    @pl.when(fold == 1)
    def _():
        c_mid.wait_recv()
        for col in range(2):
            for kk in range(HALF):
                msend[col, kk] = (mid[col, kk].astype(F32) + mid_in[col, kk].astype(F32)).astype(BF16)

        @pl.when(has_dn)
        def _():
            m_near.start()
            m_diag.start()

    c_home.wait_recv()
    for kk in range(HALF):
        hsend[kk] = (
            home[fold, 1 - side, kk].astype(F32) + home_in[1 - side, kk].astype(F32)
        ).astype(BF16)
    e_home = remote(hsend, hrecv, es.at[0], er.at[0], peer, fold)
    e_home.start()
    for kk in range(HALF):
        acc[0, :, 0:128] = home[fold, side, kk].astype(F32) + home_in[side, kk].astype(F32)
        out[kk] = acc[0, 0:LAGS, 0:128]
    e_home.wait_recv()

    def count_of(block):
        return jnp.where(block < nblk, cnt[jnp.minimum(block, nblk - 1)], 0)

    with_mid = jnp.logical_and(fold == 1, has_up)

    @pl.when(with_mid)
    def _():
        m_near.wait_recv()
        m_diag.wait_recv()
        for kk in range(HALF):
            acc[0, :, 0:128] = mrecv[0, kk].astype(F32) + mrecv[1, kk].astype(F32)
            out[kk] += acc[0, 0:LAGS, 0:128]

    for kk in range(HALF):
        k = fold * HALF + kk + 1
        pair = [jnp.minimum(cnt[2 * cable + b], count_of(2 * cable + b + k)) for b in range(2)]
        divisor = jnp.maximum(jnp.where(low, pair[0], pair[1]), 1).astype(F32)
        acc[0, :, 0:128] = hrecv[kk].astype(F32)
        out[kk] = (out[kk] + acc[0, 0:LAGS, 0:128]) / divisor

    x_mask.wait_send()
    for copy in x_raw:
        copy.wait_send()
    for q, (s, col) in enumerate([(0, own_at), (0, nb_at), (1, own_at), (1, nb_at)]):
        up, dn = chunk_copies(q, s, col)

        @pl.when(has_up)
        def _():
            up.wait_send()

        @pl.when(has_dn)
        def _():
            dn.wait_send()

    @pl.when(fold == 0)
    def _():
        c_mid.wait_send()

    c_home.wait_send()
    e_home.wait_send()

    @pl.when(jnp.logical_and(fold == 1, has_dn))
    def _():
        m_near.wait_send()
        m_diag.wait_send()


def body(size, raw, seg_count, mask):
    seg_dev, samples, chan = raw.shape
    kept = seg_dev // 2
    vmem = pl.BlockSpec(memory_space=pltpu.VMEM)
    dma = pltpu.SemaphoreType.DMA
    white = pltpu.VMEM((kept, 2, samples, 128), BF16)
    lagged = pltpu.VMEM((2, HALF, ROWS, 128), BF16)
    return pl.pallas_call(
        functools.partial(kernel, size),
        out_shape=jax.ShapeDtypeStruct((HALF, LAGS, chan), F32),
        in_specs=[
            pl.BlockSpec(memory_space=pl.ANY),
            vmem,
            pl.BlockSpec(memory_space=pltpu.SMEM),
            pl.BlockSpec(memory_space=pl.ANY),
            vmem,
        ],
        out_specs=vmem,
        scratch_shapes=[
            pltpu.VMEM((samples, samples), BF16),
            pltpu.VMEM((kept, samples, 128), BF16),
            pltpu.VMEM((kept, samples, 128), BF16),
            pltpu.VMEM((8, 128), jnp.int32),
            pltpu.VMEM((8, 128), jnp.int32),
            pltpu.VMEM((samples, 128), F32),
            pltpu.VMEM((samples // 2 + 16, 128), F32),
            white, white, white,
            pltpu.VMEM((9, samples, 256), BF16),
            pltpu.VMEM((9, ROWS, 256), F32),
            pltpu.VMEM((2, 2, HALF, ROWS, 128), BF16),
            lagged,
            lagged,
            lagged,
            pltpu.VMEM((HALF, ROWS, 128), BF16),
            lagged,
            pltpu.VMEM((HALF, ROWS, 128), BF16),
            lagged,
            dma((kept + 1,)),
            dma((kept + 1,)), dma((kept + 1,)),
            dma((4,)), dma((4,)), dma((4,)), dma((4,)),
            dma((2,)), dma((2,)),
            dma((1,)), dma((1,)),
            dma((2,)), dma((2,)),
        ],
        compiler_params=pltpu.CompilerParams(
            collective_id=0, has_side_effects=True, vmem_limit_bytes=40 * 1024 * 1024
        ),
        cost_estimate=pl.CostEstimate(flops=3 * 10**9, bytes_accessed=8 * 10**6, transcendentals=0),
    )(raw, mask.reshape(1, chan), seg_count, jnp.asarray(forward_table(samples)), jnp.asarray(lag_table(samples)))


def solution(mesh):
    in_specs = (P(("group", "fold"), None, "cable"), P("group"), P(("group", "cable")))
    out_specs = P(("group", "fold"), None, "cable")
    run = functools.partial(body, mesh.shape["cable"])
    return jax.shard_map(run, mesh=mesh, in_specs=in_specs, out_specs=out_specs, check_vma=False)
```

```python
import functools
import math

import jax
import jax.numpy as jnp
import ml_dtypes
import numpy as np
from jax import lax
from jax.experimental import pallas as pl
from jax.experimental.pallas import tpu as pltpu
from jax.sharding import PartitionSpec as P

CHAN_BLK = 64
LAGS = 101
ROWS = 112
NOFF = 8
HALF = NOFF // 2
F32 = jnp.float32
BF16 = jnp.bfloat16
MESH = pl.DeviceIdType.MESH


def forward_table(samples):
    bins = samples // 2
    phase = np.outer(np.arange(bins), np.arange(samples)) % samples * (2.0 * math.pi / samples)
    return np.concatenate([np.cos(phase), -np.sin(phase)], axis=0).astype(ml_dtypes.bfloat16)


def lag_table(samples):
    bins = samples // 2
    lag = np.arange(LAGS) - LAGS // 2 + samples
    phase = np.outer(lag, np.arange(bins)) % samples * (2.0 * math.pi / samples)
    table = np.concatenate([np.cos(phase), -np.sin(phase)], axis=1) / math.sqrt(bins)
    full = np.zeros((ROWS, samples), np.float64)
    full[:LAGS] = table
    return full.astype(ml_dtypes.bfloat16)


MID = [(0, 7), (0, 8), (1, 5), (1, 6), (1, 7), (1, 8)]
HOME = [(0, 5), (0, 6), (0, 7), (1, 5), (0, 1), (0, 2), (0, 3), (0, 4), (1, 1), (1, 2), (1, 3), (1, 4)]


def kernel(
    size,
    raw, mask_hbm, cnt_hbm, basis_hbm, inv_hbm,
    out,
    mask, cnt, inv, basis, own_raw, nb_raw, mask_out, mask_in, spec, power, w0, wu, wl, prods, acc,
    home, mid, home_in, mid_in, hsend, msend, hrecv, mrecv,
    load_sem, xs, xr, us, ur, ds, dr, cs, cr, es, er, ms, mr,
):
    samples = raw.shape[1]
    bins = samples // 2
    cable = lax.axis_index("cable")
    fold = lax.axis_index("fold")
    side = cable % 2
    node = cable // 2
    has_up = node < size // 2 - 1
    has_dn = node > 0
    peer = cable + 1 - 2 * side
    nblk = cnt.shape[0]
    seg_dev = raw.shape[0]
    kept = seg_dev // 2

    def remote(src, dst, ssem, rsem, at, core):
        return pltpu.make_async_remote_copy(
            src_ref=src, dst_ref=dst, send_sem=ssem, recv_sem=rsem,
            device_id={"cable": at, "fold": core}, device_id_type=MESH,
        )

    raw_load = [
        pltpu.make_async_copy(raw.at[kept * side + s], own_raw.at[s], load_sem.at[s])
        for s in range(kept)
    ]
    basis_load = pltpu.make_async_copy(basis_hbm, basis, load_sem.at[kept])
    mask_load = pltpu.make_async_copy(mask_hbm, mask, load_sem.at[kept + 1])
    cnt_load = pltpu.make_async_copy(cnt_hbm, cnt, load_sem.at[kept + 2])
    inv_load = pltpu.make_async_copy(inv_hbm, inv, load_sem.at[kept + 3])
    mask_load.start()
    cnt_load.start()
    raw_load[0].start()
    basis_load.start()
    for s in range(1, kept):
        raw_load[s].start()
    inv_load.start()
    mask_load.wait()
    mask_out[...] = jnp.broadcast_to(mask[...], mask_out.shape)

    barrier = pltpu.get_barrier_semaphore()

    def greet(at, core):
        pl.semaphore_signal(barrier, inc=1, device_id={"cable": at, "fold": core}, device_id_type=MESH)

    greet(peer, fold)
    greet(cable, 1 - fold)

    @pl.when(has_up)
    def _():
        greet(cable + 2, fold)
        greet(peer + 2, fold)

    @pl.when(has_dn)
    def _():
        greet(cable - 2, fold)
        greet(peer - 2, fold)

    peers = 2 + jnp.where(has_up, 2, 0) + jnp.where(has_dn, 2, 0)
    pl.semaphore_wait(barrier, peers)

    x_raw = [
        remote(raw.at[kept * (1 - side) + s], nb_raw.at[s], xs.at[s], xr.at[s], peer, fold)
        for s in range(kept)
    ]
    x_mask = remote(mask_out, mask_in, xs.at[kept], xr.at[kept], peer, fold)
    x_mask.start()
    for copy in x_raw:
        copy.start()

    power[0:8, :] = jnp.zeros((8, 128), F32)
    power[bins + 8 : bins + 16, :] = jnp.zeros((8, 128), F32)
    zero_tile = jnp.zeros((ROWS, 128), BF16)
    home[1, 0, 3] = zero_tile
    for kk in range(1, 4):
        home[1, 1, kk] = zero_tile
    mid[0, 0] = zero_tile
    mid[0, 1] = zero_tile

    @pl.when(jnp.logical_not(has_up))
    def _():
        @pl.loop(0, bins * 2 // 64)
        def _(t):
            at = pl.ds(pl.multiple_of(t * 64, 64), 64)
            for s in range(kept):
                for col in range(2):
                    wu[s, col, at, :] = jnp.zeros((64, 128), BF16)

    @pl.when(jnp.logical_not(has_dn))
    def _():
        @pl.loop(0, bins * 2 // 64)
        def _(t):
            at = pl.ds(pl.multiple_of(t * 64, 64), 64)
            for s in range(kept):
                for col in range(2):
                    wl[s, col, at, :] = jnp.zeros((64, 128), BF16)

    lane = lax.broadcasted_iota(jnp.int32, (1, 128), 1)
    low = lane < CHAN_BLK

    def whiten(source, usable, owner, s, dst):
        seg = fold * seg_dev + kept * side + s
        count = jnp.where(low, cnt[2 * owner], cnt[2 * owner + 1])
        keep = jnp.where(seg < count, usable.astype(F32), 0.0)

        def squares(t, total):
            v = source[pl.ds(pl.multiple_of(t * 64, 64), 64), :].astype(F32)
            return total + jnp.sum((v * v).reshape(8, 8, 128), axis=0)

        total = lax.fori_loop(0, samples // 64, squares, jnp.zeros((8, 128), F32))
        mean = jnp.sum(total, axis=0, keepdims=True) * (1.0 / samples)
        rate = lax.rsqrt(mean + 1e-06)
        clipped = jnp.clip(source[...].astype(F32) * rate, -2.0, 2.0).astype(BF16)

        @pl.loop(0, samples // 256)
        def _(t):
            at = pl.ds(pl.multiple_of(t * 256, 256), 256)
            spec[at, :] = jnp.dot(basis[at, :], clipped, preferred_element_type=F32)

        def powers(t, total):
            at = pl.multiple_of(t * 64, 64)
            re = spec[pl.ds(at, 64), :]
            im = spec[pl.ds(bins + at, 64), :]
            p = re * re + im * im
            power[pl.ds(8 + at, 64), :] = p
            return total + jnp.sum(p.reshape(8, 8, 128), axis=0)

        total = lax.fori_loop(0, bins // 64, powers, jnp.zeros((8, 128), F32))
        floor = jnp.sum(total, axis=0, keepdims=True) * (0.01 / bins)

        @pl.loop(0, bins // 64)
        def _(t):
            at = pl.multiple_of(t * 64, 64)
            wide = power[pl.ds(at, 80), :]
            smooth = wide[6:70] + wide[7:71] + wide[8:72] + wide[9:73] + wide[10:74]
            factor = keep * lax.rsqrt(smooth * 0.2 + floor)
            dst[pl.ds(at, 64), :] = (spec[pl.ds(at, 64), :] * factor).astype(BF16)
            dst[pl.ds(bins + at, 64), :] = (spec[pl.ds(bins + at, 64), :] * factor).astype(BF16)

    def chunk_copies(q, s, col):
        up = remote(w0.at[s, col], wl.at[s, col], us.at[q], dr.at[q], cable + 2, fold)
        dn = remote(w0.at[s, col], wu.at[s, col], ds.at[q], ur.at[q], cable - 2, fold)
        return up, dn

    def send(q, s, col):
        up, dn = chunk_copies(q, s, col)

        @pl.when(has_up)
        def _():
            up.start()

        @pl.when(has_dn)
        def _():
            dn.start()

    def arrive(q, s, col):
        up, dn = chunk_copies(q, s, col)

        @pl.when(has_dn)
        def _():
            up.wait_recv()

        @pl.when(has_up)
        def _():
            dn.wait_recv()

    def crosses(s):
        @pl.loop(0, bins // 16)
        def _(t):
            at = pl.multiple_of(t * 16, 16)

            def load(ref, col):
                return (
                    ref[s, col, pl.ds(at, 16), :].astype(F32),
                    ref[s, col, pl.ds(bins + at, 16), :].astype(F32),
                )

            e0, e1 = load(w0, 0), load(w0, 1)
            u0, u1 = load(wu, 0), load(wu, 1)
            l0, l1 = load(wl, 0), load(wl, 1)
            swap = lambda pair: tuple(pltpu.roll(v, CHAN_BLK, 1) for v in pair)
            join = lambda a, b: tuple(jnp.where(low, p, q) for p, q in zip(a, b))
            zero = (jnp.zeros((16, 128), F32),) * 2
            re0, re1, ru0, ru1 = swap(e0), swap(e1), swap(u0), swap(u1)
            o0, o1, o2, o3 = join(re0, re1), join(re1, ru0), join(ru0, ru1), join(ru1, zero)
            v0 = join(zero, ru0)
            ext = {(0, 1): o0, (0, 2): e1, (0, 3): o1, (0, 4): u0, (0, 5): o2, (0, 6): u1, (0, 7): o3,
                   (1, 1): o1, (1, 2): u0, (1, 3): o2, (1, 4): u1, (1, 5): o3}
            far = {(0, 7): v0, (0, 8): u0, (1, 5): v0, (1, 6): u0, (1, 7): o2, (1, 8): u1}
            jobs = [((l0, l1)[key[0]], far[key]) for key in MID]
            jobs += [((e0, e1)[key[0]], ext[key]) for key in HOME]
            for i, (a, b) in enumerate(jobs):
                lanes = slice(i % 2 * 128, i % 2 * 128 + 128)
                prods[i // 2, pl.ds(at, 16), lanes] = (a[0] * b[0] + a[1] * b[1]).astype(BF16)
                prods[i // 2, pl.ds(bins + at, 16), lanes] = (a[1] * b[0] - a[0] * b[1]).astype(BF16)

    def slot(i):
        if i < len(MID):
            col, k = MID[i]
            return mid.at[col, k - 1 - HALF]
        col, k = HOME[i - len(MID)]
        return home.at[(k - 1) // HALF, col, (k - 1) % HALF]

    def lags(i):
        return jnp.dot(inv[...], prods[i], preferred_element_type=F32)

    own_at, nb_at = side, 1 - side
    cnt_load.wait()
    raw_load[0].wait()
    basis_load.wait()
    whiten(own_raw.at[0], mask[...], cable, 0, w0.at[0, own_at])
    send(0, 0, own_at)
    raw_load[1].wait()
    whiten(own_raw.at[1], mask[...], cable, 1, w0.at[1, own_at])
    x_mask.wait_recv()
    x_raw[0].wait_recv()
    whiten(nb_raw.at[0], mask_in[0:1, :], peer, 0, w0.at[0, nb_at])
    send(1, 0, nb_at)
    send(2, 1, own_at)
    x_raw[1].wait_recv()
    whiten(nb_raw.at[1], mask_in[0:1, :], peer, 1, w0.at[1, nb_at])
    send(3, 1, nb_at)

    arrive(0, 0, own_at)
    arrive(1, 0, nb_at)
    crosses(0)
    inv_load.wait()
    for i in range(9):
        acc[i] = lags(i)
    arrive(2, 1, own_at)
    arrive(3, 1, nb_at)
    crosses(1)

    def finish(i):
        total = acc[i] + lags(i)
        slot(2 * i)[...] = total[:, :128].astype(BF16)
        slot(2 * i + 1)[...] = total[:, 128:].astype(BF16)

    for i in range(3):
        finish(i)
    c_mid = remote(mid, mid_in, cs.at[0], cr.at[0], cable, 1 - fold)

    @pl.when(fold == 0)
    def _():
        c_mid.start()

    for i in range(3, 9):
        finish(i)
    c_home = remote(home.at[1 - fold], home_in, cs.at[1], cr.at[1], cable, 1 - fold)
    c_home.start()

    m_near = remote(msend.at[side], mrecv.at[0], ms.at[0], mr.at[0], cable - 2, fold)
    m_diag = remote(msend.at[1 - side], mrecv.at[1], ms.at[1], mr.at[1], peer - 2, fold)

    @pl.when(fold == 1)
    def _():
        c_mid.wait_recv()
        for col in range(2):
            for kk in range(HALF):
                msend[col, kk] = (mid[col, kk].astype(F32) + mid_in[col, kk].astype(F32)).astype(BF16)

        @pl.when(has_dn)
        def _():
            m_near.start()
            m_diag.start()

    c_home.wait_recv()
    for kk in range(HALF):
        hsend[kk] = (
            home[fold, 1 - side, kk].astype(F32) + home_in[1 - side, kk].astype(F32)
        ).astype(BF16)
    e_home = remote(hsend, hrecv, es.at[0], er.at[0], peer, fold)
    e_home.start()
    for kk in range(HALF):
        acc[0, :, 0:128] = home[fold, side, kk].astype(F32) + home_in[side, kk].astype(F32)
        out[kk] = acc[0, 0:LAGS, 0:128]
    e_home.wait_recv()

    def count_of(block):
        return jnp.where(block < nblk, cnt[jnp.minimum(block, nblk - 1)], 0)

    with_mid = jnp.logical_and(fold == 1, has_up)

    @pl.when(with_mid)
    def _():
        m_near.wait_recv()
        m_diag.wait_recv()
        for kk in range(HALF):
            acc[0, :, 0:128] = mrecv[0, kk].astype(F32) + mrecv[1, kk].astype(F32)
            out[kk] += acc[0, 0:LAGS, 0:128]

    for kk in range(HALF):
        k = fold * HALF + kk + 1
        pair = [jnp.minimum(cnt[2 * cable + b], count_of(2 * cable + b + k)) for b in range(2)]
        divisor = jnp.maximum(jnp.where(low, pair[0], pair[1]), 1).astype(F32)
        acc[0, :, 0:128] = hrecv[kk].astype(F32)
        out[kk] = (out[kk] + acc[0, 0:LAGS, 0:128]) / divisor

    x_mask.wait_send()
    for copy in x_raw:
        copy.wait_send()
    for q, (s, col) in enumerate([(0, own_at), (0, nb_at), (1, own_at), (1, nb_at)]):
        up, dn = chunk_copies(q, s, col)

        @pl.when(has_up)
        def _():
            up.wait_send()

        @pl.when(has_dn)
        def _():
            dn.wait_send()

    @pl.when(fold == 0)
    def _():
        c_mid.wait_send()

    c_home.wait_send()
    e_home.wait_send()

    @pl.when(jnp.logical_and(fold == 1, has_dn))
    def _():
        m_near.wait_send()
        m_diag.wait_send()


def body(size, raw, seg_count, mask):
    seg_dev, samples, chan = raw.shape
    kept = seg_dev // 2
    vmem = pl.BlockSpec(memory_space=pltpu.VMEM)
    dma = pltpu.SemaphoreType.DMA
    white = pltpu.VMEM((kept, 2, samples, 128), BF16)
    lagged = pltpu.VMEM((2, HALF, ROWS, 128), BF16)
    return pl.pallas_call(
        functools.partial(kernel, size),
        out_shape=jax.ShapeDtypeStruct((HALF, LAGS, chan), F32),
        in_specs=[pl.BlockSpec(memory_space=pltpu.HBM)] * 5,
        out_specs=vmem,
        scratch_shapes=[
            pltpu.VMEM((1, 128), jnp.int32),
            pltpu.SMEM(seg_count.shape, jnp.int32),
            pltpu.VMEM((ROWS, samples), BF16),
            pltpu.VMEM((samples, samples), BF16),
            pltpu.VMEM((kept, samples, 128), BF16),
            pltpu.VMEM((kept, samples, 128), BF16),
            pltpu.VMEM((8, 128), jnp.int32),
            pltpu.VMEM((8, 128), jnp.int32),
            pltpu.VMEM((samples, 128), F32),
            pltpu.VMEM((samples // 2 + 16, 128), F32),
            white, white, white,
            pltpu.VMEM((9, samples, 256), BF16),
            pltpu.VMEM((9, ROWS, 256), F32),
            pltpu.VMEM((2, 2, HALF, ROWS, 128), BF16),
            lagged,
            lagged,
            lagged,
            pltpu.VMEM((HALF, ROWS, 128), BF16),
            lagged,
            pltpu.VMEM((HALF, ROWS, 128), BF16),
            lagged,
            dma((kept + 4,)),
            dma((kept + 1,)), dma((kept + 1,)),
            dma((4,)), dma((4,)), dma((4,)), dma((4,)),
            dma((2,)), dma((2,)),
            dma((1,)), dma((1,)),
            dma((2,)), dma((2,)),
        ],
        compiler_params=pltpu.CompilerParams(
            collective_id=0, has_side_effects=True, vmem_limit_bytes=40 * 1024 * 1024
        ),
        cost_estimate=pl.CostEstimate(flops=3 * 10**9, bytes_accessed=8 * 10**6, transcendentals=0),
    )(raw, mask.reshape(1, chan), seg_count, jnp.asarray(forward_table(samples)), jnp.asarray(lag_table(samples)))


def solution(mesh):
    in_specs = (P(("group", "fold"), None, "cable"), P("group"), P(("group", "cable")))
    out_specs = P(("group", "fold"), None, "cable")
    run = functools.partial(body, mesh.shape["cable"])
    return jax.shard_map(run, mesh=mesh, in_specs=in_specs, out_specs=out_specs, check_vma=False)
```

```python
import functools
import math

import jax
import jax.numpy as jnp
import ml_dtypes
import numpy as np
from jax import lax
from jax.experimental import pallas as pl
from jax.experimental.pallas import tpu as pltpu
from jax.sharding import PartitionSpec as P

CHAN_BLK = 64
LAGS = 101
ROWS = 112
NOFF = 8
HALF = NOFF // 2
PIECES = 4
F32 = jnp.float32
BF16 = jnp.bfloat16
MESH = pl.DeviceIdType.MESH


def row_order(samples):
    return np.arange(samples).reshape(2, PIECES, -1).transpose(1, 0, 2).reshape(-1)


def forward_table(samples):
    bins = samples // 2
    phase = np.outer(np.arange(bins), np.arange(samples)) % samples * (2.0 * math.pi / samples)
    table = np.concatenate([np.cos(phase), -np.sin(phase)], axis=0)
    return table[row_order(samples)].astype(ml_dtypes.bfloat16)


def lag_table(samples):
    bins = samples // 2
    lag = np.arange(LAGS) - LAGS // 2 + samples
    phase = np.outer(lag, np.arange(bins)) % samples * (2.0 * math.pi / samples)
    table = np.concatenate([np.cos(phase), -np.sin(phase)], axis=1) / math.sqrt(bins)
    full = np.zeros((ROWS, samples), np.float64)
    full[:LAGS] = table[:, row_order(samples)]
    return full.astype(ml_dtypes.bfloat16)


MID = [(0, 7), (0, 8), (1, 5), (1, 6), (1, 7), (1, 8)]
HOME = [(0, 5), (0, 6), (0, 7), (1, 5), (0, 1), (0, 2), (0, 3), (0, 4), (1, 1), (1, 2), (1, 3), (1, 4)]


def kernel(
    size,
    raw, mask_hbm, cnt_hbm, basis_hbm, inv_hbm,
    out,
    mask, cnt, inv, basis, own_raw, nb_raw, mask_out, mask_in, spec, power, w0, wu, wl, prods, acc,
    home, mid, home_in, mid_in, hsend, msend, hrecv, mrecv,
    load_sem, xs, xr, us, ur, ds, dr, cs, cr, es, er, ms, mr,
):
    samples = raw.shape[1]
    bins = samples // 2
    cable = lax.axis_index("cable")
    fold = lax.axis_index("fold")
    side = cable % 2
    node = cable // 2
    has_up = node < size // 2 - 1
    has_dn = node > 0
    peer = cable + 1 - 2 * side
    nblk = cnt.shape[0]
    seg_dev = raw.shape[0]
    kept = seg_dev // 2
    part = samples // PIECES
    part_bins = part // 2

    def rows_of(t, tile):
        per = part_bins // tile
        re = pl.multiple_of(t // per * part + t % per * tile, tile)
        return pl.ds(re, tile), pl.ds(pl.multiple_of(re + part_bins, tile), tile)

    def remote(src, dst, ssem, rsem, at, core):
        return pltpu.make_async_remote_copy(
            src_ref=src, dst_ref=dst, send_sem=ssem, recv_sem=rsem,
            device_id={"cable": at, "fold": core}, device_id_type=MESH,
        )

    raw_load = [
        pltpu.make_async_copy(raw.at[kept * side + s], own_raw.at[s], load_sem.at[s])
        for s in range(kept)
    ]
    basis_load = pltpu.make_async_copy(basis_hbm, basis, load_sem.at[kept])
    mask_load = pltpu.make_async_copy(mask_hbm, mask, load_sem.at[kept + 1])
    cnt_load = pltpu.make_async_copy(cnt_hbm, cnt, load_sem.at[kept + 2])
    inv_load = pltpu.make_async_copy(inv_hbm, inv, load_sem.at[kept + 3])
    mask_load.start()
    cnt_load.start()
    raw_load[0].start()
    basis_load.start()
    for s in range(1, kept):
        raw_load[s].start()
    inv_load.start()
    mask_load.wait()
    mask_out[...] = jnp.broadcast_to(mask[...], mask_out.shape)

    barrier = pltpu.get_barrier_semaphore()

    def greet(at, core):
        pl.semaphore_signal(barrier, inc=1, device_id={"cable": at, "fold": core}, device_id_type=MESH)

    greet(peer, fold)
    greet(cable, 1 - fold)

    @pl.when(has_up)
    def _():
        greet(cable + 2, fold)
        greet(peer + 2, fold)

    @pl.when(has_dn)
    def _():
        greet(cable - 2, fold)
        greet(peer - 2, fold)

    peers = 2 + jnp.where(has_up, 2, 0) + jnp.where(has_dn, 2, 0)
    pl.semaphore_wait(barrier, peers)

    x_raw = [
        remote(raw.at[kept * (1 - side) + s], nb_raw.at[s], xs.at[s], xr.at[s], peer, fold)
        for s in range(kept)
    ]
    x_mask = remote(mask_out, mask_in, xs.at[kept], xr.at[kept], peer, fold)
    x_mask.start()
    for copy in x_raw:
        copy.start()

    power[0:8, :] = jnp.zeros((8, 128), F32)
    power[bins + 8 : bins + 16, :] = jnp.zeros((8, 128), F32)
    zero_tile = jnp.zeros((ROWS, 128), BF16)
    home[1, 0, 3] = zero_tile
    for kk in range(1, 4):
        home[1, 1, kk] = zero_tile

    @pl.when(jnp.logical_not(has_up))
    def _():
        @pl.loop(0, bins * 2 // 64)
        def _(t):
            at = pl.ds(pl.multiple_of(t * 64, 64), 64)
            for s in range(kept):
                for col in range(2):
                    wu[s, col, at, :] = jnp.zeros((64, 128), BF16)

    @pl.when(jnp.logical_not(has_dn))
    def _():
        @pl.loop(0, bins * 2 // 64)
        def _(t):
            at = pl.ds(pl.multiple_of(t * 64, 64), 64)
            for s in range(kept):
                for col in range(2):
                    wl[s, col, at, :] = jnp.zeros((64, 128), BF16)

    lane = lax.broadcasted_iota(jnp.int32, (1, 128), 1)
    low = lane < CHAN_BLK

    def whiten(source, usable, owner, s, dst):
        seg = fold * seg_dev + kept * side + s
        count = jnp.where(low, cnt[2 * owner], cnt[2 * owner + 1])
        keep = jnp.where(seg < count, usable.astype(F32), 0.0)

        def squares(t, total):
            v = source[pl.ds(pl.multiple_of(t * 64, 64), 64), :].astype(F32)
            return total + jnp.sum((v * v).reshape(8, 8, 128), axis=0)

        total = lax.fori_loop(0, samples // 64, squares, jnp.zeros((8, 128), F32))
        mean = jnp.sum(total, axis=0, keepdims=True) * (1.0 / samples)
        rate = lax.rsqrt(mean + 1e-06)
        clipped = jnp.clip(source[...].astype(F32) * rate, -2.0, 2.0).astype(BF16)

        @pl.loop(0, samples // 256)
        def _(t):
            at = pl.ds(pl.multiple_of(t * 256, 256), 256)
            spec[at, :] = jnp.dot(basis[at, :], clipped, preferred_element_type=F32)

        def powers(t, total):
            at = pl.multiple_of(t * 64, 64)
            re_at, im_at = rows_of(t, 64)
            re = spec[re_at, :]
            im = spec[im_at, :]
            p = re * re + im * im
            power[pl.ds(8 + at, 64), :] = p
            return total + jnp.sum(p.reshape(8, 8, 128), axis=0)

        total = lax.fori_loop(0, bins // 64, powers, jnp.zeros((8, 128), F32))
        floor = jnp.sum(total, axis=0, keepdims=True) * (0.01 / bins)

        @pl.loop(0, bins // 64)
        def _(t):
            at = pl.multiple_of(t * 64, 64)
            wide = power[pl.ds(at, 80), :]
            smooth = wide[6:70] + wide[7:71] + wide[8:72] + wide[9:73] + wide[10:74]
            factor = keep * lax.rsqrt(smooth * 0.2 + floor)
            for rows in rows_of(t, 64):
                dst[rows, :] = (spec[rows, :] * factor).astype(BF16)

    own_at, nb_at = side, 1 - side
    whole = pl.ds(0, samples)
    chunks = [(0, own_at, whole), (0, nb_at, whole), (1, own_at, whole)]
    chunks += [(1, nb_at, pl.ds(p * part, part)) for p in range(PIECES)]

    def chunk_copies(q):
        at = chunks[q]
        up = remote(w0.at[at], wl.at[at], us.at[q], dr.at[q], cable + 2, fold)
        dn = remote(w0.at[at], wu.at[at], ds.at[q], ur.at[q], cable - 2, fold)
        return up, dn

    def send(q):
        up, dn = chunk_copies(q)

        @pl.when(has_up)
        def _():
            up.start()

        @pl.when(has_dn)
        def _():
            dn.start()

    def arrive(q):
        up, dn = chunk_copies(q)

        @pl.when(has_dn)
        def _():
            up.wait_recv()

        @pl.when(has_up)
        def _():
            dn.wait_recv()

    def crosses(s, first, last):
        @pl.loop(first * (part_bins // 16), last * (part_bins // 16))
        def _(t):
            re_at, im_at = rows_of(t, 16)

            def load(ref, col):
                return (
                    ref[s, col, re_at, :].astype(F32),
                    ref[s, col, im_at, :].astype(F32),
                )

            e0, e1 = load(w0, 0), load(w0, 1)
            u0, u1 = load(wu, 0), load(wu, 1)
            l0, l1 = load(wl, 0), load(wl, 1)
            swap = lambda pair: tuple(pltpu.roll(v, CHAN_BLK, 1) for v in pair)
            join = lambda a, b: tuple(jnp.where(low, p, q) for p, q in zip(a, b))
            zero = (jnp.zeros((16, 128), F32),) * 2
            re0, re1, ru0, ru1 = swap(e0), swap(e1), swap(u0), swap(u1)
            o0, o1, o2, o3 = join(re0, re1), join(re1, ru0), join(ru0, ru1), join(ru1, zero)
            v0 = join(zero, ru0)
            ext = {(0, 1): o0, (0, 2): e1, (0, 3): o1, (0, 4): u0, (0, 5): o2, (0, 6): u1, (0, 7): o3,
                   (1, 1): o1, (1, 2): u0, (1, 3): o2, (1, 4): u1, (1, 5): o3}
            far = {(0, 7): v0, (0, 8): u0, (1, 5): v0, (1, 6): u0, (1, 7): o2, (1, 8): u1}
            jobs = [((l0, l1)[key[0]], far[key]) for key in MID]
            jobs += [((e0, e1)[key[0]], ext[key]) for key in HOME]
            for i, (a, b) in enumerate(jobs):
                lanes = slice(i % 2 * 128, i % 2 * 128 + 128)
                prods[i // 2, re_at, lanes] = (a[0] * b[0] + a[1] * b[1]).astype(BF16)
                prods[i // 2, im_at, lanes] = (a[1] * b[0] - a[0] * b[1]).astype(BF16)

    def slot(i):
        if i < len(MID):
            return mid.at[i]
        col, k = HOME[i - len(MID)]
        return home.at[(k - 1) // HALF, col, (k - 1) % HALF]

    def lags(i, rows):
        return jnp.dot(inv[:, rows], prods[i, rows, :], preferred_element_type=F32)

    cnt_load.wait()
    raw_load[0].wait()
    basis_load.wait()
    whiten(own_raw.at[0], mask[...], cable, 0, w0.at[0, own_at])
    send(0)
    raw_load[1].wait()
    whiten(own_raw.at[1], mask[...], cable, 1, w0.at[1, own_at])
    x_mask.wait_recv()
    x_raw[0].wait_recv()
    whiten(nb_raw.at[0], mask_in[0:1, :], peer, 0, w0.at[0, nb_at])
    send(1)
    send(2)
    x_raw[1].wait_recv()
    whiten(nb_raw.at[1], mask_in[0:1, :], peer, 1, w0.at[1, nb_at])
    for p in range(PIECES):
        send(3 + p)

    arrive(0)
    arrive(1)
    crosses(0, 0, PIECES)
    inv_load.wait()
    for i in range(9):
        acc[i] = lags(i, slice(0, samples))
    arrive(2)

    c_mid = remote(mid, mid_in, cs.at[0], cr.at[0], cable, 1 - fold)
    for p in range(PIECES):
        arrive(3 + p)
        crosses(1, p, p + 1)
        for i in range(9):
            total = acc[i] + lags(i, slice(p * part, (p + 1) * part))
            if p < PIECES - 1:
                acc[i] = total
                continue
            slot(2 * i)[...] = total[:, :128].astype(BF16)
            slot(2 * i + 1)[...] = total[:, 128:].astype(BF16)
            if 2 * i + 2 == len(MID):

                @pl.when(fold == 0)
                def _():
                    c_mid.start()

    c_home = remote(home.at[1 - fold], home_in, cs.at[1], cr.at[1], cable, 1 - fold)
    c_home.start()

    def mid_copies():
        for at in range(2):
            tiles = (pl.ds(0, 2), pl.ds(2, 4))
            there = (pl.ds(0, 2), pl.ds(0, 4))
            near = remote(msend.at[tiles[at]], mrecv.at[0, there[at]], ms.at[0], mr.at[0], cable - 2, fold)
            diag = remote(msend.at[tiles[1 - at]], mrecv.at[1, there[1 - at]], ms.at[1], mr.at[1], peer - 2, fold)
            yield side == at, near, diag

    def home_copies():
        yield fold == 0, HALF, remote(hsend, hrecv, es.at[0], er.at[0], peer, fold)
        for at, tiles in ((0, 1), (1, 3)):
            some = pl.ds(0, tiles)
            on = jnp.logical_and(fold == 1, side == at)
            yield on, tiles, remote(hsend.at[some], hrecv.at[some], es.at[0], er.at[0], peer, fold)

    sends_mid = jnp.logical_and(fold == 1, has_dn)
    gets_mid = jnp.logical_and(fold == 1, has_up)

    @pl.when(fold == 1)
    def _():
        c_mid.wait_recv()
        for i in range(len(MID)):
            msend[i] = (mid[i].astype(F32) + mid_in[i].astype(F32)).astype(BF16)

    for on, near, diag in mid_copies():

        @pl.when(jnp.logical_and(sends_mid, on))
        def _():
            diag.start()
            near.start()

    c_home.wait_recv()
    for on, tiles, copy in home_copies():

        @pl.when(on)
        def _():
            for kk in range(tiles):
                hsend[kk] = (
                    home[fold, 1 - side, kk].astype(F32) + home_in[1 - side, kk].astype(F32)
                ).astype(BF16)
            copy.start()

    for kk in range(HALF):
        acc[kk, :, 0:128] = home[fold, side, kk].astype(F32) + home_in[side, kk].astype(F32)

    e_side = [(fold == 0, HALF, hrecv)]
    e_side += [(jnp.logical_and(fold == 1, side == at), tiles, hrecv) for at, tiles in ((0, 3), (1, 1))]
    for on, tiles, ref in e_side:

        @pl.when(on)
        def _():
            some = ref.at[pl.ds(0, tiles)]
            remote(some, some, es.at[0], er.at[0], peer, fold).wait_recv()
            for kk in range(tiles):
                acc[kk, :, 0:128] += ref[kk].astype(F32)

    for at, tiles in ((0, 2), (1, 4)):

        @pl.when(jnp.logical_and(gets_mid, side == at))
        def _():
            for j in range(2):
                some = mrecv.at[j, pl.ds(0, tiles)]
                remote(some, some, ms.at[j], mr.at[j], peer, fold).wait_recv()
            for i in range(tiles):
                acc[HALF - tiles + i, :, 0:128] += mrecv[0, i].astype(F32) + mrecv[1, i].astype(F32)

    def count_of(block):
        return jnp.where(block < nblk, cnt[jnp.minimum(block, nblk - 1)], 0)

    for kk in range(HALF):
        k = fold * HALF + kk + 1
        pair = [jnp.minimum(cnt[2 * cable + b], count_of(2 * cable + b + k)) for b in range(2)]
        divisor = jnp.maximum(jnp.where(low, pair[0], pair[1]), 1).astype(F32)
        out[pl.ds(kk, LAGS, stride=HALF), :] = acc[kk, 0:LAGS, 0:128] / divisor

    x_mask.wait_send()
    for copy in x_raw:
        copy.wait_send()
    for q in range(len(chunks)):
        up, dn = chunk_copies(q)

        @pl.when(has_up)
        def _():
            up.wait_send()

        @pl.when(has_dn)
        def _():
            dn.wait_send()

    @pl.when(fold == 0)
    def _():
        c_mid.wait_send()

    c_home.wait_send()
    for on, tiles, copy in home_copies():

        @pl.when(on)
        def _():
            copy.wait_send()

    for on, near, diag in mid_copies():

        @pl.when(jnp.logical_and(sends_mid, on))
        def _():
            near.wait_send()
            diag.wait_send()


def body(size, raw, seg_count, mask):
    seg_dev, samples, chan = raw.shape
    kept = seg_dev // 2
    vmem = pl.BlockSpec(memory_space=pltpu.VMEM)
    dma = pltpu.SemaphoreType.DMA
    white = pltpu.VMEM((kept, 2, samples, 128), BF16)
    lagged = pltpu.VMEM((2, HALF, ROWS, 128), BF16)
    mids = pltpu.VMEM((len(MID), ROWS, 128), BF16)
    lagged_sums = pl.pallas_call(
        functools.partial(kernel, size),
        out_shape=jax.ShapeDtypeStruct((LAGS * HALF, chan), F32),
        in_specs=[pl.BlockSpec(memory_space=pltpu.HBM)] * 5,
        out_specs=vmem,
        scratch_shapes=[
            pltpu.VMEM((1, 128), jnp.int32),
            pltpu.SMEM(seg_count.shape, jnp.int32),
            pltpu.VMEM((ROWS, samples), BF16),
            pltpu.VMEM((samples, samples), BF16),
            pltpu.VMEM((kept, samples, 128), BF16),
            pltpu.VMEM((kept, samples, 128), BF16),
            pltpu.VMEM((8, 128), jnp.int32),
            pltpu.VMEM((8, 128), jnp.int32),
            pltpu.VMEM((samples, 128), F32),
            pltpu.VMEM((samples // 2 + 16, 128), F32),
            white, white, white,
            pltpu.VMEM((9, samples, 256), BF16),
            pltpu.VMEM((9, ROWS, 256), F32),
            pltpu.VMEM((2, 2, HALF, ROWS, 128), BF16),
            mids,
            lagged,
            mids,
            pltpu.VMEM((HALF, ROWS, 128), BF16),
            mids,
            pltpu.VMEM((HALF, ROWS, 128), BF16),
            lagged,
            dma((kept + 4,)),
            dma((kept + 1,)), dma((kept + 1,)),
            dma((3 + PIECES,)), dma((3 + PIECES,)), dma((3 + PIECES,)), dma((3 + PIECES,)),
            dma((2,)), dma((2,)),
            dma((1,)), dma((1,)),
            dma((2,)), dma((2,)),
        ],
        compiler_params=pltpu.CompilerParams(
            collective_id=0, has_side_effects=True, vmem_limit_bytes=63 * 1024 * 1024
        ),
        cost_estimate=pl.CostEstimate(flops=3 * 10**9, bytes_accessed=8 * 10**6, transcendentals=0),
    )(raw, mask.reshape(1, chan), seg_count, jnp.asarray(forward_table(samples)), jnp.asarray(lag_table(samples)))
    return lagged_sums.reshape(LAGS, HALF, chan).transpose(1, 0, 2)


def solution(mesh):
    in_specs = (P(("group", "fold"), None, "cable"), P("group"), P(("group", "cable")))
    out_specs = P(("group", "fold"), None, "cable")
    run = functools.partial(body, mesh.shape["cable"])
    return jax.shard_map(run, mesh=mesh, in_specs=in_specs, out_specs=out_specs, check_vma=False)
```

```python
import functools
import math

import jax
import jax.numpy as jnp
import ml_dtypes
import numpy as np
from jax import lax
from jax.experimental import pallas as pl
from jax.experimental.pallas import tpu as pltpu
from jax.sharding import PartitionSpec as P

CHAN_BLK = 64
LAGS = 101
ROWS = 112
NOFF = 8
HALF = NOFF // 2
PIECES = 4
F32 = jnp.float32
BF16 = jnp.bfloat16
MESH = pl.DeviceIdType.MESH


def row_order(samples):
    return np.arange(samples).reshape(2, PIECES, -1).transpose(1, 0, 2).reshape(-1)


def forward_table(samples):
    bins = samples // 2
    phase = np.outer(np.arange(bins), np.arange(samples)) % samples * (2.0 * math.pi / samples)
    table = np.concatenate([np.cos(phase), -np.sin(phase)], axis=0)
    return table[row_order(samples)].astype(ml_dtypes.bfloat16)


def lag_table(samples):
    bins = samples // 2
    lag = np.arange(LAGS) - LAGS // 2 + samples
    phase = np.outer(lag, np.arange(bins)) % samples * (2.0 * math.pi / samples)
    table = np.concatenate([np.cos(phase), -np.sin(phase)], axis=1) / math.sqrt(bins)
    full = np.zeros((ROWS, samples), np.float64)
    full[:LAGS] = table[:, row_order(samples)]
    return full.astype(ml_dtypes.bfloat16)


MID = [(0, 7), (0, 8), (1, 5), (1, 6), (1, 7), (1, 8)]
HOME = [(0, 5), (0, 6), (0, 7), (1, 5), (0, 1), (0, 2), (0, 3), (0, 4), (1, 1), (1, 2), (1, 3), (1, 4)]


def kernel(
    size,
    raw, mask_hbm, cnt_hbm, basis_hbm, inv_hbm,
    out,
    mask, cnt, inv, basis, own_raw, nb_raw, mask_out, mask_in, spec, power, w0, wu, wl, prods, acc,
    home, mid, home_in, mid_in, hsend, msend, hrecv, mrecv,
    load_sem, xs, xr, us, ur, ds, dr, cs, cr, es, er, ms, mr,
):
    samples = raw.shape[1]
    bins = samples // 2
    cable = lax.axis_index("cable")
    fold = lax.axis_index("fold")
    side = cable % 2
    node = cable // 2
    has_up = node < size // 2 - 1
    has_dn = node > 0
    peer = cable + 1 - 2 * side
    nblk = cnt.shape[0]
    seg_dev = raw.shape[0]
    kept = seg_dev // 2
    part = samples // PIECES
    part_bins = part // 2

    def rows_of(t, tile):
        per = part_bins // tile
        re = pl.multiple_of(t // per * part + t % per * tile, tile)
        return pl.ds(re, tile), pl.ds(pl.multiple_of(re + part_bins, tile), tile)

    def remote(src, dst, ssem, rsem, at, core):
        return pltpu.make_async_remote_copy(
            src_ref=src, dst_ref=dst, send_sem=ssem, recv_sem=rsem,
            device_id={"cable": at, "fold": core}, device_id_type=MESH,
        )

    barrier = pltpu.get_barrier_semaphore()

    def greet(at, core):
        pl.semaphore_signal(barrier, inc=1, device_id={"cable": at, "fold": core}, device_id_type=MESH)

    greet(peer, fold)
    greet(cable, 1 - fold)

    @pl.when(has_up)
    def _():
        greet(cable + 2, fold)
        greet(peer + 2, fold)

    @pl.when(has_dn)
    def _():
        greet(cable - 2, fold)
        greet(peer - 2, fold)

    raw_load = [
        pltpu.make_async_copy(raw.at[kept * side + s], own_raw.at[s], load_sem.at[s])
        for s in range(kept)
    ]
    basis_load = pltpu.make_async_copy(basis_hbm, basis, load_sem.at[kept])
    mask_load = pltpu.make_async_copy(mask_hbm, mask, load_sem.at[kept + 1])
    cnt_load = pltpu.make_async_copy(cnt_hbm, cnt, load_sem.at[kept + 2])
    inv_load = pltpu.make_async_copy(inv_hbm, inv, load_sem.at[kept + 3])
    mask_load.start()
    cnt_load.start()
    raw_load[0].start()
    basis_load.start()
    for s in range(1, kept):
        raw_load[s].start()
    inv_load.start()
    mask_load.wait()
    mask_out[...] = jnp.broadcast_to(mask[...], mask_out.shape)

    power[0:8, :] = jnp.zeros((8, 128), F32)
    power[bins + 8 : bins + 16, :] = jnp.zeros((8, 128), F32)
    zero_tile = jnp.zeros((ROWS, 128), BF16)
    home[1, 0, 3] = zero_tile
    for kk in range(1, 4):
        home[1, 1, kk] = zero_tile

    @pl.when(jnp.logical_not(has_up))
    def _():
        @pl.loop(0, bins * 2 // 64)
        def _(t):
            at = pl.ds(pl.multiple_of(t * 64, 64), 64)
            for s in range(kept):
                for col in range(2):
                    wu[s, col, at, :] = jnp.zeros((64, 128), BF16)

    @pl.when(jnp.logical_not(has_dn))
    def _():
        @pl.loop(0, bins * 2 // 64)
        def _(t):
            at = pl.ds(pl.multiple_of(t * 64, 64), 64)
            for s in range(kept):
                for col in range(2):
                    wl[s, col, at, :] = jnp.zeros((64, 128), BF16)

    lane = lax.broadcasted_iota(jnp.int32, (1, 128), 1)
    low = lane < CHAN_BLK

    def whiten(source, usable, owner, s, dst):
        seg = fold * seg_dev + kept * side + s
        count = jnp.where(low, cnt[2 * owner], cnt[2 * owner + 1])
        keep = jnp.where(seg < count, usable.astype(F32), 0.0)

        def squares(t, total):
            v = source[pl.ds(pl.multiple_of(t * 64, 64), 64), :].astype(F32)
            return total + jnp.sum((v * v).reshape(8, 8, 128), axis=0)

        total = lax.fori_loop(0, samples // 64, squares, jnp.zeros((8, 128), F32))
        mean = jnp.sum(total, axis=0, keepdims=True) * (1.0 / samples)
        rate = lax.rsqrt(mean + 1e-06)
        clipped = jnp.clip(source[...].astype(F32) * rate, -2.0, 2.0).astype(BF16)

        @pl.loop(0, samples // 256)
        def _(t):
            at = pl.ds(pl.multiple_of(t * 256, 256), 256)
            spec[at, :] = jnp.dot(basis[at, :], clipped, preferred_element_type=F32)

        def powers(t, total):
            at = pl.multiple_of(t * 64, 64)
            re_at, im_at = rows_of(t, 64)
            re = spec[re_at, :]
            im = spec[im_at, :]
            p = re * re + im * im
            power[pl.ds(8 + at, 64), :] = p
            return total + jnp.sum(p.reshape(8, 8, 128), axis=0)

        total = lax.fori_loop(0, bins // 64, powers, jnp.zeros((8, 128), F32))
        floor = jnp.sum(total, axis=0, keepdims=True) * (0.01 / bins)

        @pl.loop(0, bins // 64)
        def _(t):
            at = pl.multiple_of(t * 64, 64)
            wide = power[pl.ds(at, 80), :]
            smooth = wide[6:70] + wide[7:71] + wide[8:72] + wide[9:73] + wide[10:74]
            factor = keep * lax.rsqrt(smooth * 0.2 + floor)
            for rows in rows_of(t, 64):
                dst[rows, :] = (spec[rows, :] * factor).astype(BF16)

    own_at, nb_at = side, 1 - side
    whole = pl.ds(0, samples)
    chunks = [(0, own_at, whole), (0, nb_at, whole), (1, own_at, whole)]
    chunks += [(1, nb_at, pl.ds(p * part, part)) for p in range(PIECES)]

    def chunk_copies(q):
        at = chunks[q]
        up = remote(w0.at[at], wl.at[at], us.at[q], dr.at[q], cable + 2, fold)
        dn = remote(w0.at[at], wu.at[at], ds.at[q], ur.at[q], cable - 2, fold)
        return up, dn

    def send(q):
        up, dn = chunk_copies(q)

        @pl.when(has_up)
        def _():
            up.start()

        @pl.when(has_dn)
        def _():
            dn.start()

    def arrive(q):
        up, dn = chunk_copies(q)

        @pl.when(has_dn)
        def _():
            up.wait_recv()

        @pl.when(has_up)
        def _():
            dn.wait_recv()

    def crosses(s, first, last):
        @pl.loop(first * (part_bins // 16), last * (part_bins // 16))
        def _(t):
            re_at, im_at = rows_of(t, 16)

            def load(ref, col):
                return (
                    ref[s, col, re_at, :].astype(F32),
                    ref[s, col, im_at, :].astype(F32),
                )

            e0, e1 = load(w0, 0), load(w0, 1)
            u0, u1 = load(wu, 0), load(wu, 1)
            l0, l1 = load(wl, 0), load(wl, 1)
            swap = lambda pair: tuple(pltpu.roll(v, CHAN_BLK, 1) for v in pair)
            join = lambda a, b: tuple(jnp.where(low, p, q) for p, q in zip(a, b))
            zero = (jnp.zeros((16, 128), F32),) * 2
            re0, re1, ru0, ru1 = swap(e0), swap(e1), swap(u0), swap(u1)
            o0, o1, o2, o3 = join(re0, re1), join(re1, ru0), join(ru0, ru1), join(ru1, zero)
            v0 = join(zero, ru0)
            ext = {(0, 1): o0, (0, 2): e1, (0, 3): o1, (0, 4): u0, (0, 5): o2, (0, 6): u1, (0, 7): o3,
                   (1, 1): o1, (1, 2): u0, (1, 3): o2, (1, 4): u1, (1, 5): o3}
            far = {(0, 7): v0, (0, 8): u0, (1, 5): v0, (1, 6): u0, (1, 7): o2, (1, 8): u1}
            jobs = [((l0, l1)[key[0]], far[key]) for key in MID]
            jobs += [((e0, e1)[key[0]], ext[key]) for key in HOME]
            for i, (a, b) in enumerate(jobs):
                lanes = slice(i % 2 * 128, i % 2 * 128 + 128)
                prods[i // 2, re_at, lanes] = (a[0] * b[0] + a[1] * b[1]).astype(BF16)
                prods[i // 2, im_at, lanes] = (a[1] * b[0] - a[0] * b[1]).astype(BF16)

    def slot(i):
        if i < len(MID):
            return mid.at[i]
        col, k = HOME[i - len(MID)]
        return home.at[(k - 1) // HALF, col, (k - 1) % HALF]

    def lags(i, rows):
        return jnp.dot(inv[:, rows], prods[i, rows, :], preferred_element_type=F32)

    cnt_load.wait()
    raw_load[0].wait()
    basis_load.wait()
    whiten(own_raw.at[0], mask[...], cable, 0, w0.at[0, own_at])
    peers = 2 + jnp.where(has_up, 2, 0) + jnp.where(has_dn, 2, 0)
    pl.semaphore_wait(barrier, peers)
    x_raw = [
        remote(raw.at[kept * (1 - side) + s], nb_raw.at[s], xs.at[s], xr.at[s], peer, fold)
        for s in range(kept)
    ]
    x_mask = remote(mask_out, mask_in, xs.at[kept], xr.at[kept], peer, fold)
    x_mask.start()
    for copy in x_raw:
        copy.start()
    send(0)
    raw_load[1].wait()
    whiten(own_raw.at[1], mask[...], cable, 1, w0.at[1, own_at])
    x_mask.wait_recv()
    x_raw[0].wait_recv()
    whiten(nb_raw.at[0], mask_in[0:1, :], peer, 0, w0.at[0, nb_at])
    send(1)
    send(2)
    x_raw[1].wait_recv()
    whiten(nb_raw.at[1], mask_in[0:1, :], peer, 1, w0.at[1, nb_at])
    for p in range(PIECES):
        send(3 + p)

    arrive(0)
    arrive(1)
    crosses(0, 0, PIECES)
    inv_load.wait()
    for i in range(9):
        acc[i] = lags(i, slice(0, samples))
    arrive(2)

    c_mid = remote(mid, mid_in, cs.at[0], cr.at[0], cable, 1 - fold)
    for p in range(PIECES):
        arrive(3 + p)
        crosses(1, p, p + 1)
        for i in range(9):
            total = acc[i] + lags(i, slice(p * part, (p + 1) * part))
            if p < PIECES - 1:
                acc[i] = total
                continue
            slot(2 * i)[...] = total[:, :128].astype(BF16)
            slot(2 * i + 1)[...] = total[:, 128:].astype(BF16)
            if 2 * i + 2 == len(MID):

                @pl.when(fold == 0)
                def _():
                    c_mid.start()

    c_home = remote(home.at[1 - fold], home_in, cs.at[1], cr.at[1], cable, 1 - fold)
    c_home.start()

    def mid_copies():
        for at in range(2):
            tiles = (pl.ds(0, 2), pl.ds(2, 4))
            there = (pl.ds(0, 2), pl.ds(0, 4))
            near = remote(msend.at[tiles[at]], mrecv.at[0, there[at]], ms.at[0], mr.at[0], cable - 2, fold)
            diag = remote(msend.at[tiles[1 - at]], mrecv.at[1, there[1 - at]], ms.at[1], mr.at[1], peer - 2, fold)
            yield side == at, near, diag

    def home_copies():
        yield fold == 0, HALF, remote(hsend, hrecv, es.at[0], er.at[0], peer, fold)
        for at, tiles in ((0, 1), (1, 3)):
            some = pl.ds(0, tiles)
            on = jnp.logical_and(fold == 1, side == at)
            yield on, tiles, remote(hsend.at[some], hrecv.at[some], es.at[0], er.at[0], peer, fold)

    sends_mid = jnp.logical_and(fold == 1, has_dn)
    gets_mid = jnp.logical_and(fold == 1, has_up)

    @pl.when(fold == 1)
    def _():
        c_mid.wait_recv()
        for i in range(len(MID)):
            msend[i] = (mid[i].astype(F32) + mid_in[i].astype(F32)).astype(BF16)

    for on, near, diag in mid_copies():

        @pl.when(jnp.logical_and(sends_mid, on))
        def _():
            diag.start()
            near.start()

    c_home.wait_recv()
    for on, tiles, copy in home_copies():

        @pl.when(on)
        def _():
            for kk in range(tiles):
                hsend[kk] = (
                    home[fold, 1 - side, kk].astype(F32) + home_in[1 - side, kk].astype(F32)
                ).astype(BF16)
            copy.start()

    for kk in range(HALF):
        acc[kk, :, 0:128] = home[fold, side, kk].astype(F32) + home_in[side, kk].astype(F32)

    e_side = [(fold == 0, HALF, hrecv)]
    e_side += [(jnp.logical_and(fold == 1, side == at), tiles, hrecv) for at, tiles in ((0, 3), (1, 1))]
    for on, tiles, ref in e_side:

        @pl.when(on)
        def _():
            some = ref.at[pl.ds(0, tiles)]
            remote(some, some, es.at[0], er.at[0], peer, fold).wait_recv()
            for kk in range(tiles):
                acc[kk, :, 0:128] += ref[kk].astype(F32)

    for at, tiles in ((0, 2), (1, 4)):

        @pl.when(jnp.logical_and(gets_mid, side == at))
        def _():
            for j in range(2):
                some = mrecv.at[j, pl.ds(0, tiles)]
                remote(some, some, ms.at[j], mr.at[j], peer, fold).wait_recv()
            for i in range(tiles):
                acc[HALF - tiles + i, :, 0:128] += mrecv[0, i].astype(F32) + mrecv[1, i].astype(F32)

    def count_of(block):
        return jnp.where(block < nblk, cnt[jnp.minimum(block, nblk - 1)], 0)

    for kk in range(HALF):
        k = fold * HALF + kk + 1
        pair = [jnp.minimum(cnt[2 * cable + b], count_of(2 * cable + b + k)) for b in range(2)]
        divisor = jnp.maximum(jnp.where(low, pair[0], pair[1]), 1).astype(F32)
        out[kk] = acc[kk, 0:LAGS, 0:128] / divisor

    x_mask.wait_send()
    for copy in x_raw:
        copy.wait_send()
    for q in range(len(chunks)):
        up, dn = chunk_copies(q)

        @pl.when(has_up)
        def _():
            up.wait_send()

        @pl.when(has_dn)
        def _():
            dn.wait_send()

    @pl.when(fold == 0)
    def _():
        c_mid.wait_send()

    c_home.wait_send()
    for on, tiles, copy in home_copies():

        @pl.when(on)
        def _():
            copy.wait_send()

    for on, near, diag in mid_copies():

        @pl.when(jnp.logical_and(sends_mid, on))
        def _():
            near.wait_send()
            diag.wait_send()


def body(size, raw, seg_count, mask):
    seg_dev, samples, chan = raw.shape
    kept = seg_dev // 2
    vmem = pl.BlockSpec(memory_space=pltpu.VMEM)
    dma = pltpu.SemaphoreType.DMA
    white = pltpu.VMEM((kept, 2, samples, 128), BF16)
    lagged = pltpu.VMEM((2, HALF, ROWS, 128), BF16)
    mids = pltpu.VMEM((len(MID), ROWS, 128), BF16)
    lagged_sums = pl.pallas_call(
        functools.partial(kernel, size),
        out_shape=jax.ShapeDtypeStruct((HALF, LAGS, chan), F32),
        in_specs=[pl.BlockSpec(memory_space=pltpu.HBM)] * 5,
        out_specs=vmem,
        scratch_shapes=[
            pltpu.VMEM((1, 128), jnp.int32),
            pltpu.SMEM(seg_count.shape, jnp.int32),
            pltpu.VMEM((ROWS, samples), BF16),
            pltpu.VMEM((samples, samples), BF16),
            pltpu.VMEM((kept, samples, 128), BF16),
            pltpu.VMEM((kept, samples, 128), BF16),
            pltpu.VMEM((8, 128), jnp.int32),
            pltpu.VMEM((8, 128), jnp.int32),
            pltpu.VMEM((samples, 128), F32),
            pltpu.VMEM((samples // 2 + 16, 128), F32),
            white, white, white,
            pltpu.VMEM((9, samples, 256), BF16),
            pltpu.VMEM((9, ROWS, 256), F32),
            pltpu.VMEM((2, 2, HALF, ROWS, 128), BF16),
            mids,
            lagged,
            mids,
            pltpu.VMEM((HALF, ROWS, 128), BF16),
            mids,
            pltpu.VMEM((HALF, ROWS, 128), BF16),
            lagged,
            dma((kept + 4,)),
            dma((kept + 1,)), dma((kept + 1,)),
            dma((3 + PIECES,)), dma((3 + PIECES,)), dma((3 + PIECES,)), dma((3 + PIECES,)),
            dma((2,)), dma((2,)),
            dma((1,)), dma((1,)),
            dma((2,)), dma((2,)),
        ],
        compiler_params=pltpu.CompilerParams(
            collective_id=0, has_side_effects=True, vmem_limit_bytes=63 * 1024 * 1024
        ),
        cost_estimate=pl.CostEstimate(flops=3 * 10**9, bytes_accessed=8 * 10**6, transcendentals=0),
    )(raw, mask.reshape(1, chan), seg_count, jnp.asarray(forward_table(samples)), jnp.asarray(lag_table(samples)))
    return lagged_sums


def solution(mesh):
    in_specs = (P(("group", "fold"), None, "cable"), P("group"), P(("group", "cable")))
    out_specs = P(("group", "fold"), None, "cable")
    run = functools.partial(body, mesh.shape["cable"])
    return jax.shard_map(run, mesh=mesh, in_specs=in_specs, out_specs=out_specs, check_vma=False)
```

```python
import functools
import math

import jax
import jax.numpy as jnp
import ml_dtypes
import numpy as np
from jax import lax
from jax.experimental import pallas as pl
from jax.experimental.pallas import tpu as pltpu
from jax.sharding import PartitionSpec as P

CHAN_BLK = 64
LAGS = 101
ROWS = 112
NOFF = 8
HALF = NOFF // 2
PIECES = 4
F32 = jnp.float32
BF16 = jnp.bfloat16
MESH = pl.DeviceIdType.MESH


def row_order(samples):
    return np.arange(samples).reshape(2, PIECES, -1).transpose(1, 0, 2).reshape(-1)


def forward_table(samples):
    bins = samples // 2
    phase = np.outer(np.arange(bins), np.arange(samples)) % samples * (2.0 * math.pi / samples)
    table = np.concatenate([np.cos(phase), -np.sin(phase)], axis=0)
    return table[row_order(samples)].astype(ml_dtypes.bfloat16)


def lag_table(samples):
    bins = samples // 2
    lag = np.arange(LAGS) - LAGS // 2 + samples
    phase = np.outer(lag, np.arange(bins)) % samples * (2.0 * math.pi / samples)
    table = np.concatenate([np.cos(phase), -np.sin(phase)], axis=1) / math.sqrt(bins)
    full = np.zeros((ROWS, samples), np.float64)
    full[:LAGS] = table[:, row_order(samples)]
    return full.astype(ml_dtypes.bfloat16)


MID = [(0, 7), (0, 8), (1, 5), (1, 6), (1, 7), (1, 8)]
HOME = [(0, 5), (0, 6), (0, 7), (1, 5), (0, 1), (0, 2), (0, 3), (0, 4), (1, 1), (1, 2), (1, 3), (1, 4)]


def kernel(
    size,
    raw, mask_hbm, cnt_hbm, basis_hbm, inv_hbm,
    out,
    mask, cnt, inv, basis, own_raw, nb_raw, mask_out, mask_in, spec, power, w0, wu, wl, prods, acc,
    home, mid, home_in, mid_in, hsend, msend, hrecv, mrecv,
    load_sem, xs, xr, us, ur, ds, dr, cs, cr, es, er, ms, mr,
):
    samples = raw.shape[1]
    bins = samples // 2
    cable = lax.axis_index("cable")
    fold = lax.axis_index("fold")
    side = cable % 2
    node = cable // 2
    has_up = node < size // 2 - 1
    has_dn = node > 0
    peer = cable + 1 - 2 * side
    nblk = cnt.shape[0]
    seg_dev = raw.shape[0]
    kept = seg_dev // 2
    part = samples // PIECES
    part_bins = part // 2

    def rows_of(t, tile):
        per = part_bins // tile
        re = pl.multiple_of(t // per * part + t % per * tile, tile)
        return pl.ds(re, tile), pl.ds(pl.multiple_of(re + part_bins, tile), tile)

    def remote(src, dst, ssem, rsem, at, core):
        return pltpu.make_async_remote_copy(
            src_ref=src, dst_ref=dst, send_sem=ssem, recv_sem=rsem,
            device_id={"cable": at, "fold": core}, device_id_type=MESH,
        )

    barrier = pltpu.get_barrier_semaphore()

    def greet(at, core):
        pl.semaphore_signal(barrier, inc=1, device_id={"cable": at, "fold": core}, device_id_type=MESH)

    greet(peer, fold)
    greet(cable, 1 - fold)

    @pl.when(has_up)
    def _():
        greet(cable + 2, fold)
        greet(peer + 2, fold)

    @pl.when(has_dn)
    def _():
        greet(cable - 2, fold)
        greet(peer - 2, fold)

    raw_load = [
        pltpu.make_async_copy(raw.at[kept * side + s], own_raw.at[s], load_sem.at[s])
        for s in range(kept)
    ]
    basis_load = pltpu.make_async_copy(basis_hbm, basis, load_sem.at[kept])
    mask_load = pltpu.make_async_copy(mask_hbm, mask, load_sem.at[kept + 1])
    cnt_load = pltpu.make_async_copy(cnt_hbm, cnt, load_sem.at[kept + 2])
    inv_load = pltpu.make_async_copy(inv_hbm, inv, load_sem.at[kept + 3])
    mask_load.start()
    cnt_load.start()
    raw_load[0].start()
    basis_load.start()
    for s in range(1, kept):
        raw_load[s].start()
    inv_load.start()
    mask_load.wait()
    mask_out[...] = jnp.broadcast_to(mask[...], mask_out.shape)

    peers = 2 + jnp.where(has_up, 2, 0) + jnp.where(has_dn, 2, 0)
    pl.semaphore_wait(barrier, peers)

    x_raw = [
        remote(raw.at[kept * (1 - side) + s], nb_raw.at[s], xs.at[s], xr.at[s], peer, fold)
        for s in range(kept)
    ]
    x_mask = remote(mask_out, mask_in, xs.at[kept], xr.at[kept], peer, fold)
    x_mask.start()
    for copy in x_raw:
        copy.start()

    power[0:8, :] = jnp.zeros((8, 128), F32)
    power[bins + 8 : bins + 16, :] = jnp.zeros((8, 128), F32)
    zero_tile = jnp.zeros((ROWS, 128), BF16)
    home[1, 0, 3] = zero_tile
    for kk in range(1, 4):
        home[1, 1, kk] = zero_tile

    @pl.when(jnp.logical_not(has_up))
    def _():
        @pl.loop(0, bins * 2 // 64)
        def _(t):
            at = pl.ds(pl.multiple_of(t * 64, 64), 64)
            for s in range(kept):
                for col in range(2):
                    wu[s, col, at, :] = jnp.zeros((64, 128), BF16)

    @pl.when(jnp.logical_not(has_dn))
    def _():
        @pl.loop(0, bins * 2 // 64)
        def _(t):
            at = pl.ds(pl.multiple_of(t * 64, 64), 64)
            for s in range(kept):
                for col in range(2):
                    wl[s, col, at, :] = jnp.zeros((64, 128), BF16)

    lane = lax.broadcasted_iota(jnp.int32, (1, 128), 1)
    low = lane < CHAN_BLK

    def whiten(source, usable, owner, s, dst):
        seg = fold * seg_dev + kept * side + s
        count = jnp.where(low, cnt[2 * owner], cnt[2 * owner + 1])
        keep = jnp.where(seg < count, usable.astype(F32), 0.0)

        def squares(t, total):
            v = source[pl.ds(pl.multiple_of(t * 64, 64), 64), :].astype(F32)
            return total + jnp.sum((v * v).reshape(8, 8, 128), axis=0)

        total = lax.fori_loop(0, samples // 64, squares, jnp.zeros((8, 128), F32))
        mean = jnp.sum(total, axis=0, keepdims=True) * (1.0 / samples)
        rate = lax.rsqrt(mean + 1e-06)
        clipped = jnp.clip(source[...].astype(F32) * rate, -2.0, 2.0).astype(BF16)

        @pl.loop(0, samples // 256)
        def _(t):
            at = pl.ds(pl.multiple_of(t * 256, 256), 256)
            spec[at, :] = jnp.dot(basis[at, :], clipped, preferred_element_type=F32)

        def powers(t, total):
            at = pl.multiple_of(t * 64, 64)
            re_at, im_at = rows_of(t, 64)
            re = spec[re_at, :]
            im = spec[im_at, :]
            p = re * re + im * im
            power[pl.ds(8 + at, 64), :] = p
            return total + jnp.sum(p.reshape(8, 8, 128), axis=0)

        total = lax.fori_loop(0, bins // 64, powers, jnp.zeros((8, 128), F32))
        floor = jnp.sum(total, axis=0, keepdims=True) * (0.01 / bins)

        @pl.loop(0, bins // 64)
        def _(t):
            at = pl.multiple_of(t * 64, 64)
            wide = power[pl.ds(at, 80), :]
            smooth = wide[6:70] + wide[7:71] + wide[8:72] + wide[9:73] + wide[10:74]
            factor = keep * lax.rsqrt(smooth * 0.2 + floor)
            for rows in rows_of(t, 64):
                dst[rows, :] = (spec[rows, :] * factor).astype(BF16)

    own_at, nb_at = side, 1 - side
    whole = pl.ds(0, samples)
    chunks = [(0, own_at, whole), (0, nb_at, whole), (1, own_at, whole)]
    chunks += [(1, nb_at, pl.ds(p * part, part)) for p in range(PIECES)]

    def chunk_copies(q):
        at = chunks[q]
        up = remote(w0.at[at], wl.at[at], us.at[q], dr.at[q], cable + 2, fold)
        dn = remote(w0.at[at], wu.at[at], ds.at[q], ur.at[q], cable - 2, fold)
        return up, dn

    def send(q):
        up, dn = chunk_copies(q)

        @pl.when(has_up)
        def _():
            up.start()

        @pl.when(has_dn)
        def _():
            dn.start()

    def arrive(q):
        up, dn = chunk_copies(q)

        @pl.when(has_dn)
        def _():
            up.wait_recv()

        @pl.when(has_up)
        def _():
            dn.wait_recv()

    def crosses(s, first, last):
        @pl.loop(first * (part_bins // 16), last * (part_bins // 16))
        def _(t):
            re_at, im_at = rows_of(t, 16)

            def load(ref, col):
                return (
                    ref[s, col, re_at, :].astype(F32),
                    ref[s, col, im_at, :].astype(F32),
                )

            e0, e1 = load(w0, 0), load(w0, 1)
            u0, u1 = load(wu, 0), load(wu, 1)
            l0, l1 = load(wl, 0), load(wl, 1)
            swap = lambda pair: tuple(pltpu.roll(v, CHAN_BLK, 1) for v in pair)
            join = lambda a, b: tuple(jnp.where(low, p, q) for p, q in zip(a, b))
            zero = (jnp.zeros((16, 128), F32),) * 2
            re0, re1, ru0, ru1 = swap(e0), swap(e1), swap(u0), swap(u1)
            o0, o1, o2, o3 = join(re0, re1), join(re1, ru0), join(ru0, ru1), join(ru1, zero)
            v0 = join(zero, ru0)
            ext = {(0, 1): o0, (0, 2): e1, (0, 3): o1, (0, 4): u0, (0, 5): o2, (0, 6): u1, (0, 7): o3,
                   (1, 1): o1, (1, 2): u0, (1, 3): o2, (1, 4): u1, (1, 5): o3}
            far = {(0, 7): v0, (0, 8): u0, (1, 5): v0, (1, 6): u0, (1, 7): o2, (1, 8): u1}
            jobs = [((l0, l1)[key[0]], far[key]) for key in MID]
            jobs += [((e0, e1)[key[0]], ext[key]) for key in HOME]
            for i, (a, b) in enumerate(jobs):
                lanes = slice(i % 2 * 128, i % 2 * 128 + 128)
                prods[i // 2, re_at, lanes] = (a[0] * b[0] + a[1] * b[1]).astype(BF16)
                prods[i // 2, im_at, lanes] = (a[1] * b[0] - a[0] * b[1]).astype(BF16)

    def slot(i):
        if i < len(MID):
            return mid.at[i]
        col, k = HOME[i - len(MID)]
        return home.at[(k - 1) // HALF, col, (k - 1) % HALF]

    def lags(i, rows):
        return jnp.dot(inv[:, rows], prods[i, rows, :], preferred_element_type=F32)

    cnt_load.wait()
    raw_load[0].wait()
    basis_load.wait()
    whiten(own_raw.at[0], mask[...], cable, 0, w0.at[0, own_at])
    send(0)
    raw_load[1].wait()
    whiten(own_raw.at[1], mask[...], cable, 1, w0.at[1, own_at])
    x_mask.wait_recv()
    x_raw[0].wait_recv()
    whiten(nb_raw.at[0], mask_in[0:1, :], peer, 0, w0.at[0, nb_at])
    send(1)
    send(2)
    x_raw[1].wait_recv()
    whiten(nb_raw.at[1], mask_in[0:1, :], peer, 1, w0.at[1, nb_at])
    for p in range(PIECES):
        send(3 + p)

    arrive(0)
    arrive(1)
    crosses(0, 0, PIECES)
    inv_load.wait()
    for i in range(9):
        acc[i] = lags(i, slice(0, samples))
    arrive(2)

    c_mid = remote(mid, mid_in, cs.at[0], cr.at[0], cable, 1 - fold)
    for p in range(PIECES):
        arrive(3 + p)
        crosses(1, p, p + 1)
        for i in range(9):
            total = acc[i] + lags(i, slice(p * part, (p + 1) * part))
            if p < PIECES - 1:
                acc[i] = total
                continue
            slot(2 * i)[...] = total[:, :128].astype(BF16)
            slot(2 * i + 1)[...] = total[:, 128:].astype(BF16)
            if 2 * i + 2 == len(MID):

                @pl.when(fold == 0)
                def _():
                    c_mid.start()

    c_home = remote(home.at[1 - fold], home_in, cs.at[1], cr.at[1], cable, 1 - fold)
    c_home.start()

    def mid_copies():
        for at in range(2):
            tiles = (pl.ds(0, 2), pl.ds(2, 4))
            there = (pl.ds(0, 2), pl.ds(0, 4))
            near = remote(msend.at[tiles[at]], mrecv.at[0, there[at]], ms.at[0], mr.at[0], cable - 2, fold)
            diag = remote(msend.at[tiles[1 - at]], mrecv.at[1, there[1 - at]], ms.at[1], mr.at[1], peer - 2, fold)
            yield side == at, near, diag

    def home_copies():
        yield fold == 0, HALF, remote(hsend, hrecv, es.at[0], er.at[0], peer, fold)
        for at, tiles in ((0, 1), (1, 3)):
            some = pl.ds(0, tiles)
            on = jnp.logical_and(fold == 1, side == at)
            yield on, tiles, remote(hsend.at[some], hrecv.at[some], es.at[0], er.at[0], peer, fold)

    sends_mid = jnp.logical_and(fold == 1, has_dn)
    gets_mid = jnp.logical_and(fold == 1, has_up)

    @pl.when(fold == 1)
    def _():
        c_mid.wait_recv()
        for i in range(len(MID)):
            msend[i] = (mid[i].astype(F32) + mid_in[i].astype(F32)).astype(BF16)

    for on, near, diag in mid_copies():

        @pl.when(jnp.logical_and(sends_mid, on))
        def _():
            diag.start()
            near.start()

    c_home.wait_recv()
    for on, tiles, copy in home_copies():

        @pl.when(on)
        def _():
            for kk in range(tiles):
                hsend[kk] = (
                    home[fold, 1 - side, kk].astype(F32) + home_in[1 - side, kk].astype(F32)
                ).astype(BF16)
            copy.start()

    for kk in range(HALF):
        acc[kk, :, 0:128] = home[fold, side, kk].astype(F32) + home_in[side, kk].astype(F32)

    e_side = [(fold == 0, HALF, hrecv)]
    e_side += [(jnp.logical_and(fold == 1, side == at), tiles, hrecv) for at, tiles in ((0, 3), (1, 1))]
    for on, tiles, ref in e_side:

        @pl.when(on)
        def _():
            some = ref.at[pl.ds(0, tiles)]
            remote(some, some, es.at[0], er.at[0], peer, fold).wait_recv()
            for kk in range(tiles):
                acc[kk, :, 0:128] += ref[kk].astype(F32)

    for at, tiles in ((0, 2), (1, 4)):

        @pl.when(jnp.logical_and(gets_mid, side == at))
        def _():
            for j in range(2):
                some = mrecv.at[j, pl.ds(0, tiles)]
                remote(some, some, ms.at[j], mr.at[j], peer, fold).wait_recv()
            for i in range(tiles):
                acc[HALF - tiles + i, :, 0:128] += mrecv[0, i].astype(F32) + mrecv[1, i].astype(F32)

    def count_of(block):
        return jnp.where(block < nblk, cnt[jnp.minimum(block, nblk - 1)], 0)

    for kk in range(HALF):
        k = fold * HALF + kk + 1
        pair = [jnp.minimum(cnt[2 * cable + b], count_of(2 * cable + b + k)) for b in range(2)]
        divisor = jnp.maximum(jnp.where(low, pair[0], pair[1]), 1).astype(F32)
        out[kk] = acc[kk, 0:LAGS, 0:128] / divisor

    x_mask.wait_send()
    for copy in x_raw:
        copy.wait_send()
    for q in range(len(chunks)):
        up, dn = chunk_copies(q)

        @pl.when(has_up)
        def _():
            up.wait_send()

        @pl.when(has_dn)
        def _():
            dn.wait_send()

    @pl.when(fold == 0)
    def _():
        c_mid.wait_send()

    c_home.wait_send()
    for on, tiles, copy in home_copies():

        @pl.when(on)
        def _():
            copy.wait_send()

    for on, near, diag in mid_copies():

        @pl.when(jnp.logical_and(sends_mid, on))
        def _():
            near.wait_send()
            diag.wait_send()


def body(size, raw, seg_count, mask):
    seg_dev, samples, chan = raw.shape
    kept = seg_dev // 2
    vmem = pl.BlockSpec(memory_space=pltpu.VMEM)
    dma = pltpu.SemaphoreType.DMA
    white = pltpu.VMEM((kept, 2, samples, 128), BF16)
    lagged = pltpu.VMEM((2, HALF, ROWS, 128), BF16)
    mids = pltpu.VMEM((len(MID), ROWS, 128), BF16)
    lagged_sums = pl.pallas_call(
        functools.partial(kernel, size),
        out_shape=jax.ShapeDtypeStruct((HALF, LAGS, chan), F32),
        in_specs=[pl.BlockSpec(memory_space=pltpu.HBM)] * 5,
        out_specs=vmem,
        scratch_shapes=[
            pltpu.VMEM((1, 128), jnp.int32),
            pltpu.SMEM(seg_count.shape, jnp.int32),
            pltpu.VMEM((ROWS, samples), BF16),
            pltpu.VMEM((samples, samples), BF16),
            pltpu.VMEM((kept, samples, 128), BF16),
            pltpu.VMEM((kept, samples, 128), BF16),
            pltpu.VMEM((8, 128), jnp.int32),
            pltpu.VMEM((8, 128), jnp.int32),
            pltpu.VMEM((samples, 128), F32),
            pltpu.VMEM((samples // 2 + 16, 128), F32),
            white, white, white,
            pltpu.VMEM((9, samples, 256), BF16),
            pltpu.VMEM((9, ROWS, 256), F32),
            pltpu.VMEM((2, 2, HALF, ROWS, 128), BF16),
            mids,
            lagged,
            mids,
            pltpu.VMEM((HALF, ROWS, 128), BF16),
            mids,
            pltpu.VMEM((HALF, ROWS, 128), BF16),
            lagged,
            dma((kept + 4,)),
            dma((kept + 1,)), dma((kept + 1,)),
            dma((3 + PIECES,)), dma((3 + PIECES,)), dma((3 + PIECES,)), dma((3 + PIECES,)),
            dma((2,)), dma((2,)),
            dma((1,)), dma((1,)),
            dma((2,)), dma((2,)),
        ],
        compiler_params=pltpu.CompilerParams(
            collective_id=0, has_side_effects=True, vmem_limit_bytes=63 * 1024 * 1024
        ),
        cost_estimate=pl.CostEstimate(flops=3 * 10**9, bytes_accessed=8 * 10**6, transcendentals=0),
    )(raw, mask.reshape(1, chan), seg_count, jnp.asarray(forward_table(samples)), jnp.asarray(lag_table(samples)))
    return lagged_sums


def solution(mesh):
    in_specs = (P(("group", "fold"), None, "cable"), P("group"), P(("group", "cable")))
    out_specs = P(("group", "fold"), None, "cable")
    run = functools.partial(body, mesh.shape["cable"])
    return jax.shard_map(run, mesh=mesh, in_specs=in_specs, out_specs=out_specs, check_vma=False)
```

```python
import functools
import math

import jax
import jax.numpy as jnp
import ml_dtypes
import numpy as np
from jax import lax
from jax.experimental import pallas as pl
from jax.experimental.pallas import tpu as pltpu
from jax.sharding import PartitionSpec as P

CHAN_BLK = 64
LAGS = 101
ROWS = 112
NOFF = 8
HALF = NOFF // 2
PIECES = 4
F32 = jnp.float32
BF16 = jnp.bfloat16
MESH = pl.DeviceIdType.MESH


def row_order(samples):
    return np.arange(samples).reshape(2, PIECES, -1).transpose(1, 0, 2).reshape(-1)


def forward_table(samples):
    bins = samples // 2
    phase = np.outer(np.arange(bins), np.arange(samples)) % samples * (2.0 * math.pi / samples)
    table = np.concatenate([np.cos(phase), -np.sin(phase)], axis=0)
    return table[row_order(samples)].astype(ml_dtypes.bfloat16)


def lag_table(samples):
    bins = samples // 2
    lag = np.arange(LAGS) - LAGS // 2 + samples
    phase = np.outer(lag, np.arange(bins)) % samples * (2.0 * math.pi / samples)
    table = np.concatenate([np.cos(phase), -np.sin(phase)], axis=1) / math.sqrt(bins)
    full = np.zeros((ROWS, samples), np.float64)
    full[:LAGS] = table[:, row_order(samples)]
    return full.astype(ml_dtypes.bfloat16)


MID = [(0, 7), (0, 8), (1, 5), (1, 6), (1, 7), (1, 8)]
HOME = [(0, 5), (0, 6), (0, 7), (1, 5), (0, 1), (0, 2), (0, 3), (0, 4), (1, 1), (1, 2), (1, 3), (1, 4)]


def kernel(
    size,
    raw, mask_hbm, cnt_hbm, basis_hbm, inv_hbm,
    out,
    mask, cnt, inv, basis, own_raw, nb_raw, mask_out, mask_in, spec, power, w0, wu, wl, prods, acc,
    home, mid, home_in, mid_in, hsend, msend, hrecv, mrecv,
    load_sem, xs, xr, us, ur, ds, dr, cs, cr, es, er, ms, mr,
):
    samples = raw.shape[1]
    bins = samples // 2
    cable = lax.axis_index("cable")
    fold = lax.axis_index("fold")
    side = cable % 2
    node = cable // 2
    has_up = node < size // 2 - 1
    has_dn = node > 0
    peer = cable + 1 - 2 * side
    nblk = cnt.shape[0]
    seg_dev = raw.shape[0]
    kept = seg_dev // 2
    part = samples // PIECES
    part_bins = part // 2

    def rows_of(t, tile):
        per = part_bins // tile
        re = pl.multiple_of(t // per * part + t % per * tile, tile)
        return pl.ds(re, tile), pl.ds(pl.multiple_of(re + part_bins, tile), tile)

    def remote(src, dst, ssem, rsem, at, core):
        return pltpu.make_async_remote_copy(
            src_ref=src, dst_ref=dst, send_sem=ssem, recv_sem=rsem,
            device_id={"cable": at, "fold": core}, device_id_type=MESH,
        )

    barrier = pltpu.get_barrier_semaphore()

    def greet(at, core):
        pl.semaphore_signal(barrier, inc=1, device_id={"cable": at, "fold": core}, device_id_type=MESH)

    greet(peer, fold)
    greet(cable, 1 - fold)

    @pl.when(has_up)
    def _():
        greet(cable + 2, fold)
        greet(peer + 2, fold)

    @pl.when(has_dn)
    def _():
        greet(cable - 2, fold)
        greet(peer - 2, fold)

    raw_load = [
        pltpu.make_async_copy(raw.at[kept * side + s], own_raw.at[s], load_sem.at[s])
        for s in range(kept)
    ]
    basis_load = pltpu.make_async_copy(basis_hbm, basis, load_sem.at[kept])
    mask_load = pltpu.make_async_copy(mask_hbm, mask, load_sem.at[kept + 1])
    cnt_load = pltpu.make_async_copy(cnt_hbm, cnt, load_sem.at[kept + 2])
    inv_load = pltpu.make_async_copy(inv_hbm, inv, load_sem.at[kept + 3])
    mask_load.start()
    cnt_load.start()
    raw_load[0].start()
    basis_load.start()
    for s in range(1, kept):
        raw_load[s].start()
    inv_load.start()
    mask_load.wait()
    mask_out[...] = jnp.broadcast_to(mask[...], mask_out.shape)

    peers = 2 + jnp.where(has_up, 2, 0) + jnp.where(has_dn, 2, 0)
    pl.semaphore_wait(barrier, peers)

    x_raw = [
        remote(raw.at[kept * (1 - side) + s], nb_raw.at[s], xs.at[s], xr.at[s], peer, fold)
        for s in range(kept)
    ]
    x_mask = remote(mask_out, mask_in, xs.at[kept], xr.at[kept], peer, fold)
    x_mask.start()
    for copy in x_raw:
        copy.start()

    power[0:8, :] = jnp.zeros((8, 128), F32)
    power[bins + 8 : bins + 16, :] = jnp.zeros((8, 128), F32)
    zero_tile = jnp.zeros((ROWS, 128), BF16)
    home[1, 0, 3] = zero_tile
    for kk in range(1, 4):
        home[1, 1, kk] = zero_tile

    @pl.when(jnp.logical_not(has_up))
    def _():
        @pl.loop(0, bins * 2 // 64)
        def _(t):
            at = pl.ds(pl.multiple_of(t * 64, 64), 64)
            for s in range(kept):
                for col in range(2):
                    wu[s, col, at, :] = jnp.zeros((64, 128), BF16)

    @pl.when(jnp.logical_not(has_dn))
    def _():
        @pl.loop(0, bins * 2 // 64)
        def _(t):
            at = pl.ds(pl.multiple_of(t * 64, 64), 64)
            for s in range(kept):
                for col in range(2):
                    wl[s, col, at, :] = jnp.zeros((64, 128), BF16)

    lane = lax.broadcasted_iota(jnp.int32, (1, 128), 1)
    low = lane < CHAN_BLK

    def whiten(source, usable, owner, s, dst):
        seg = fold * seg_dev + kept * side + s
        count = jnp.where(low, cnt[2 * owner], cnt[2 * owner + 1])
        keep = jnp.where(seg < count, usable.astype(F32), 0.0)

        def squares(t, total):
            v = source[pl.ds(pl.multiple_of(t * 64, 64), 64), :].astype(F32)
            return total + jnp.sum((v * v).reshape(8, 8, 128), axis=0)

        total = lax.fori_loop(0, samples // 64, squares, jnp.zeros((8, 128), F32))
        mean = jnp.sum(total, axis=0, keepdims=True) * (1.0 / samples)
        rate = lax.rsqrt(mean + 1e-06)
        clipped = jnp.clip(source[...].astype(F32) * rate, -2.0, 2.0).astype(BF16)

        @pl.loop(0, samples // 256)
        def _(t):
            at = pl.ds(pl.multiple_of(t * 256, 256), 256)
            spec[at, :] = jnp.dot(basis[at, :], clipped, preferred_element_type=F32)

        def powers(t, total):
            at = pl.multiple_of(t * 64, 64)
            re_at, im_at = rows_of(t, 64)
            re = spec[re_at, :]
            im = spec[im_at, :]
            p = re * re + im * im
            power[pl.ds(8 + at, 64), :] = p
            return total + jnp.sum(p.reshape(8, 8, 128), axis=0)

        total = lax.fori_loop(0, bins // 64, powers, jnp.zeros((8, 128), F32))
        floor = jnp.sum(total, axis=0, keepdims=True) * (0.01 / bins)

        @pl.loop(0, bins // 64)
        def _(t):
            at = pl.multiple_of(t * 64, 64)
            wide = power[pl.ds(at, 80), :]
            smooth = wide[6:70] + wide[7:71] + wide[8:72] + wide[9:73] + wide[10:74]
            factor = keep * lax.rsqrt(smooth * 0.2 + floor)
            for rows in rows_of(t, 64):
                dst[rows, :] = (spec[rows, :] * factor).astype(BF16)

    own_at, nb_at = side, 1 - side
    whole = pl.ds(0, samples)
    chunks = [(0, own_at, whole), (0, nb_at, whole), (1, own_at, whole)]
    chunks += [(1, nb_at, pl.ds(p * part, part)) for p in range(PIECES)]

    def chunk_copies(q):
        at = chunks[q]
        up = remote(w0.at[at], wl.at[at], us.at[q], dr.at[q], cable + 2, fold)
        dn = remote(w0.at[at], wu.at[at], ds.at[q], ur.at[q], cable - 2, fold)
        return up, dn

    def send(q):
        up, dn = chunk_copies(q)

        @pl.when(has_up)
        def _():
            up.start()

        @pl.when(has_dn)
        def _():
            dn.start()

    def arrive(q):
        up, dn = chunk_copies(q)

        @pl.when(has_dn)
        def _():
            up.wait_recv()

        @pl.when(has_up)
        def _():
            dn.wait_recv()

    def crosses(s, first, last):
        @pl.loop(first * (part_bins // 16), last * (part_bins // 16))
        def _(t):
            re_at, im_at = rows_of(t, 16)

            def load(ref, col):
                return (
                    ref[s, col, re_at, :].astype(F32),
                    ref[s, col, im_at, :].astype(F32),
                )

            e0, e1 = load(w0, 0), load(w0, 1)
            u0, u1 = load(wu, 0), load(wu, 1)
            l0, l1 = load(wl, 0), load(wl, 1)
            swap = lambda pair: tuple(pltpu.roll(v, CHAN_BLK, 1) for v in pair)
            join = lambda a, b: tuple(jnp.where(low, p, q) for p, q in zip(a, b))
            zero = (jnp.zeros((16, 128), F32),) * 2
            re0, re1, ru0, ru1 = swap(e0), swap(e1), swap(u0), swap(u1)
            o0, o1, o2, o3 = join(re0, re1), join(re1, ru0), join(ru0, ru1), join(ru1, zero)
            v0 = join(zero, ru0)
            ext = {(0, 1): o0, (0, 2): e1, (0, 3): o1, (0, 4): u0, (0, 5): o2, (0, 6): u1, (0, 7): o3,
                   (1, 1): o1, (1, 2): u0, (1, 3): o2, (1, 4): u1, (1, 5): o3}
            far = {(0, 7): v0, (0, 8): u0, (1, 5): v0, (1, 6): u0, (1, 7): o2, (1, 8): u1}
            jobs = [((l0, l1)[key[0]], far[key]) for key in MID]
            jobs += [((e0, e1)[key[0]], ext[key]) for key in HOME]
            for i, (a, b) in enumerate(jobs):
                lanes = slice(i % 2 * 128, i % 2 * 128 + 128)
                prods[i // 2, re_at, lanes] = (a[0] * b[0] + a[1] * b[1]).astype(BF16)
                prods[i // 2, im_at, lanes] = (a[1] * b[0] - a[0] * b[1]).astype(BF16)

    def slot(i):
        if i < len(MID):
            return mid.at[i]
        col, k = HOME[i - len(MID)]
        return home.at[(k - 1) // HALF, col, (k - 1) % HALF]

    def lags(i, rows):
        return jnp.dot(inv[:, rows], prods[i, rows, :], preferred_element_type=F32)

    cnt_load.wait()
    raw_load[0].wait()
    basis_load.wait()
    whiten(own_raw.at[0], mask[...], cable, 0, w0.at[0, own_at])
    send(0)
    raw_load[1].wait()
    whiten(own_raw.at[1], mask[...], cable, 1, w0.at[1, own_at])
    send(2)
    x_mask.wait_recv()
    x_raw[0].wait_recv()
    whiten(nb_raw.at[0], mask_in[0:1, :], peer, 0, w0.at[0, nb_at])
    send(1)
    x_raw[1].wait_recv()
    whiten(nb_raw.at[1], mask_in[0:1, :], peer, 1, w0.at[1, nb_at])
    for p in range(PIECES):
        send(3 + p)

    arrive(0)
    arrive(1)
    crosses(0, 0, PIECES)
    inv_load.wait()
    for i in range(9):
        acc[i] = lags(i, slice(0, samples))
    arrive(2)

    c_mid = remote(mid, mid_in, cs.at[0], cr.at[0], cable, 1 - fold)
    for p in range(PIECES):
        arrive(3 + p)
        crosses(1, p, p + 1)
        for i in range(9):
            total = acc[i] + lags(i, slice(p * part, (p + 1) * part))
            if p < PIECES - 1:
                acc[i] = total
                continue
            slot(2 * i)[...] = total[:, :128].astype(BF16)
            slot(2 * i + 1)[...] = total[:, 128:].astype(BF16)
            if 2 * i + 2 == len(MID):

                @pl.when(fold == 0)
                def _():
                    c_mid.start()

    c_home = remote(home.at[1 - fold], home_in, cs.at[1], cr.at[1], cable, 1 - fold)
    c_home.start()

    def mid_copies():
        for at in range(2):
            tiles = (pl.ds(0, 2), pl.ds(2, 4))
            there = (pl.ds(0, 2), pl.ds(0, 4))
            near = remote(msend.at[tiles[at]], mrecv.at[0, there[at]], ms.at[0], mr.at[0], cable - 2, fold)
            diag = remote(msend.at[tiles[1 - at]], mrecv.at[1, there[1 - at]], ms.at[1], mr.at[1], peer - 2, fold)
            yield side == at, near, diag

    def home_copies():
        yield fold == 0, HALF, remote(hsend, hrecv, es.at[0], er.at[0], peer, fold)
        for at, tiles in ((0, 1), (1, 3)):
            some = pl.ds(0, tiles)
            on = jnp.logical_and(fold == 1, side == at)
            yield on, tiles, remote(hsend.at[some], hrecv.at[some], es.at[0], er.at[0], peer, fold)

    sends_mid = jnp.logical_and(fold == 1, has_dn)
    gets_mid = jnp.logical_and(fold == 1, has_up)

    @pl.when(fold == 1)
    def _():
        c_mid.wait_recv()
        for i in range(len(MID)):
            msend[i] = (mid[i].astype(F32) + mid_in[i].astype(F32)).astype(BF16)

    for on, near, diag in mid_copies():

        @pl.when(jnp.logical_and(sends_mid, on))
        def _():
            diag.start()
            near.start()

    c_home.wait_recv()
    for on, tiles, copy in home_copies():

        @pl.when(on)
        def _():
            for kk in range(tiles):
                hsend[kk] = (
                    home[fold, 1 - side, kk].astype(F32) + home_in[1 - side, kk].astype(F32)
                ).astype(BF16)
            copy.start()

    for kk in range(HALF):
        acc[kk, :, 0:128] = home[fold, side, kk].astype(F32) + home_in[side, kk].astype(F32)

    e_side = [(fold == 0, HALF, hrecv)]
    e_side += [(jnp.logical_and(fold == 1, side == at), tiles, hrecv) for at, tiles in ((0, 3), (1, 1))]
    for on, tiles, ref in e_side:

        @pl.when(on)
        def _():
            some = ref.at[pl.ds(0, tiles)]
            remote(some, some, es.at[0], er.at[0], peer, fold).wait_recv()
            for kk in range(tiles):
                acc[kk, :, 0:128] += ref[kk].astype(F32)

    for at, tiles in ((0, 2), (1, 4)):

        @pl.when(jnp.logical_and(gets_mid, side == at))
        def _():
            for j in range(2):
                some = mrecv.at[j, pl.ds(0, tiles)]
                remote(some, some, ms.at[j], mr.at[j], peer, fold).wait_recv()
            for i in range(tiles):
                acc[HALF - tiles + i, :, 0:128] += mrecv[0, i].astype(F32) + mrecv[1, i].astype(F32)

    def count_of(block):
        return jnp.where(block < nblk, cnt[jnp.minimum(block, nblk - 1)], 0)

    for kk in range(HALF):
        k = fold * HALF + kk + 1
        pair = [jnp.minimum(cnt[2 * cable + b], count_of(2 * cable + b + k)) for b in range(2)]
        divisor = jnp.maximum(jnp.where(low, pair[0], pair[1]), 1).astype(F32)
        out[kk] = acc[kk, 0:LAGS, 0:128] / divisor

    x_mask.wait_send()
    for copy in x_raw:
        copy.wait_send()
    for q in range(len(chunks)):
        up, dn = chunk_copies(q)

        @pl.when(has_up)
        def _():
            up.wait_send()

        @pl.when(has_dn)
        def _():
            dn.wait_send()

    @pl.when(fold == 0)
    def _():
        c_mid.wait_send()

    c_home.wait_send()
    for on, tiles, copy in home_copies():

        @pl.when(on)
        def _():
            copy.wait_send()

    for on, near, diag in mid_copies():

        @pl.when(jnp.logical_and(sends_mid, on))
        def _():
            near.wait_send()
            diag.wait_send()


def body(size, raw, seg_count, mask):
    seg_dev, samples, chan = raw.shape
    kept = seg_dev // 2
    vmem = pl.BlockSpec(memory_space=pltpu.VMEM)
    dma = pltpu.SemaphoreType.DMA
    white = pltpu.VMEM((kept, 2, samples, 128), BF16)
    lagged = pltpu.VMEM((2, HALF, ROWS, 128), BF16)
    mids = pltpu.VMEM((len(MID), ROWS, 128), BF16)
    lagged_sums = pl.pallas_call(
        functools.partial(kernel, size),
        out_shape=jax.ShapeDtypeStruct((HALF, LAGS, chan), F32),
        in_specs=[pl.BlockSpec(memory_space=pltpu.HBM)] * 5,
        out_specs=vmem,
        scratch_shapes=[
            pltpu.VMEM((1, 128), jnp.int32),
            pltpu.SMEM(seg_count.shape, jnp.int32),
            pltpu.VMEM((ROWS, samples), BF16),
            pltpu.VMEM((samples, samples), BF16),
            pltpu.VMEM((kept, samples, 128), BF16),
            pltpu.VMEM((kept, samples, 128), BF16),
            pltpu.VMEM((8, 128), jnp.int32),
            pltpu.VMEM((8, 128), jnp.int32),
            pltpu.VMEM((samples, 128), F32),
            pltpu.VMEM((samples // 2 + 16, 128), F32),
            white, white, white,
            pltpu.VMEM((9, samples, 256), BF16),
            pltpu.VMEM((9, ROWS, 256), F32),
            pltpu.VMEM((2, 2, HALF, ROWS, 128), BF16),
            mids,
            lagged,
            mids,
            pltpu.VMEM((HALF, ROWS, 128), BF16),
            mids,
            pltpu.VMEM((HALF, ROWS, 128), BF16),
            lagged,
            dma((kept + 4,)),
            dma((kept + 1,)), dma((kept + 1,)),
            dma((3 + PIECES,)), dma((3 + PIECES,)), dma((3 + PIECES,)), dma((3 + PIECES,)),
            dma((2,)), dma((2,)),
            dma((1,)), dma((1,)),
            dma((2,)), dma((2,)),
        ],
        compiler_params=pltpu.CompilerParams(
            collective_id=0, has_side_effects=True, vmem_limit_bytes=63 * 1024 * 1024
        ),
        cost_estimate=pl.CostEstimate(flops=3 * 10**9, bytes_accessed=8 * 10**6, transcendentals=0),
    )(raw, mask.reshape(1, chan), seg_count, jnp.asarray(forward_table(samples)), jnp.asarray(lag_table(samples)))
    return lagged_sums


def solution(mesh):
    in_specs = (P(("group", "fold"), None, "cable"), P("group"), P(("group", "cable")))
    out_specs = P(("group", "fold"), None, "cable")
    run = functools.partial(body, mesh.shape["cable"])
    return jax.shard_map(run, mesh=mesh, in_specs=in_specs, out_specs=out_specs, check_vma=False)
```
